256 devices in a mesh: sp: 32 (over x, y, core), tp: 8 (over z).
Axes of the slice: x: 4, y: 4, z: 8, core: 2. Of those that a mesh axis runs over, the one named last changes fastest.
Arguments:
- queries: bfloat16 [16384, 8192], P('sp', 'tp'), may hold values from -200 to 200
- keys: bfloat16 [16384, 1024], P('sp', 'tp'), may hold values from -6 to 6
- values: bfloat16 [16384, 1024], P('sp', 'tp'), may hold values from -6 to 6
- w_out: bfloat16 [8192, 4096], P('tp'), may hold values from -0.0625 to 0.0625
- lengths: int32 [4], replicated, may hold values from 1 to 4096
- stretch_owner: int32 [32], replicated, may hold values from 0 to 31, as said below
- home_replica: int32 [4], replicated, may hold values from 0 to 31, as said below
Outputs:
- mixed: bfloat16 [16384, 4096], P(('sp', 'tp'))
- cache_keys: bfloat16 [131072, 1024], P('sp', 'tp')
- home_cache_values: bfloat16 [131072, 1024], P('sp', 'tp')
The draws below stay inside these ranges and needn't reach their ends.
Inputs may be any that keep to these rules, and one draw needn't show every extreme that they name: Stretch c of prompt p stands on replica stretch_owner[p * 8 + c]; every replica appears once. `home_replica`: the prompts' home replicas are distinct; prompt 0's home is (stretch_owner[0] + 32 / 2) modulo 32.
All inputs are finite; a program needn't handle non-finite values.
Results may differ from the reference program's by a relative error of at most 0.014.
Values may be sent and summed in bfloat16 or wider, within the bound.
No kernel may reach another device: no remote copies, remote signals or barrier semaphores. Data moves between devices by JAX's collectives and lax.ppermute only.
A program may use at most 128 MiB of HBM per device.

```python
import jax
import jax.numpy as jnp
from jax import lax

D = 4096
HEADS = 64
KV_HEADS = 8
HEAD_DIM = 128
STRETCH = 512
MAX_STRETCHES = 8
PROMPTS = 4
TOKENS = 16384
CACHE_ROWS = 131072
N_SP = 32
N_TP = 8


def pair_draw(key):
    base = jax.random.fold_in(key, 11)
    key_part, query_part = jax.random.split(base, 2)
    key_rows = jnp.clip(jax.random.normal(key_part, (TOKENS, KV_HEADS * HEAD_DIM), jnp.float32), -6.0, 6.0)
    query_rows = jnp.clip(jax.random.normal(query_part, (TOKENS, HEADS * HEAD_DIM), jnp.float32), -6.0, 6.0)
    return (query_rows, key_rows)


def draw_queries(key, part):
    return pair_draw(key)[0].astype(jnp.bfloat16)


def draw_keys(key, part):
    return pair_draw(key)[1].astype(jnp.bfloat16)


def placement_draw(key):
    owner_list = jax.random.permutation(jax.random.fold_in(key, 7), N_SP).astype(jnp.int32)
    first_home = (owner_list[0] + N_SP // 2) % N_SP
    shuffled = jax.random.permutation(jax.random.fold_in(key, 5), N_SP).astype(jnp.int32)
    order_index = jnp.argsort((shuffled == first_home).astype(jnp.int32), stable=True)
    remaining = shuffled[order_index]
    homes = jnp.concatenate([first_home[None], remaining[:PROMPTS - 1]], 0).astype(jnp.int32)
    return (owner_list, homes)


def draw_stretch_owner(key, part):
    return placement_draw(key)[0]


def draw_home_replica(key, part):
    return placement_draw(key)[1]


def touch_ends(entries, own_key, least, high):
    shape = entries.shape
    index_at = [jax.random.randint(jax.random.fold_in(own_key, axis), (), 0, shape[axis]) for axis in range(len(shape))]
    entries = entries.at[tuple(index_at)].set(least)
    longest = shape.index(max(shape))
    index_at[longest] = (index_at[longest] + 1) % shape[longest]
    return entries.at[tuple(index_at)].set(high)


def block_levels(own_key, shape, cuts, least, high):
    loudness, own = 1.0, jax.random.fold_in(own_key, 6)
    for position, parts in cuts:
        steps = jnp.exp(jax.random.uniform(jax.random.fold_in(own, position), (parts,), jnp.float32, least / len(cuts), high / len(cuts)))
        loudness = loudness * jnp.repeat(steps, shape[position] // parts).reshape([-1 if axis == position else 1 for axis in range(len(shape))])
    return loudness


def bell_draw(key, extent, deviation, reach, shards=(), held_as=jnp.bfloat16):
    values = jax.random.normal(key, extent, jnp.float32) * deviation
    if len(shards) > 0:
        values = block_levels(key, extent, shards, -0.22, 0.18) * values
    return jnp.clip(values, min=-reach, max=reach).astype(held_as)


def setup_inputs(seed: int = 0) -> dict:
    arg_keys = jax.random.split(jax.random.key(seed), 8)
    return {
        "queries": draw_queries(jax.random.fold_in(arg_keys[7], 71), 0),
        "keys": draw_keys(jax.random.fold_in(arg_keys[7], 71), 0),
        "values": bell_draw(arg_keys[2], (TOKENS, KV_HEADS * HEAD_DIM), 1.0, 6.0, ((0, 32), (1, 8))),
        "w_out": bell_draw(arg_keys[3], (HEADS * HEAD_DIM, D), (HEADS * HEAD_DIM) ** -0.5, 0.0625, ((0, 8),)),
        "lengths": touch_ends(jax.random.randint(arg_keys[4], (PROMPTS,), 1, MAX_STRETCHES * STRETCH + 1), jax.random.fold_in(arg_keys[4], 1), 1, MAX_STRETCHES * STRETCH).astype(jnp.int32),
        "stretch_owner": draw_stretch_owner(jax.random.fold_in(arg_keys[7], 71), 0),
        "home_replica": draw_home_replica(jax.random.fold_in(arg_keys[7], 71), 0),
    }


def reference(queries, keys, values, w_out, lengths, stretch_owner, home_replica):
    group_size = HEADS // KV_HEADS
    score_scale = HEAD_DIM ** -0.5
    cache_span = MAX_STRETCHES * STRETCH
    positions = jnp.arange(cache_span, dtype=jnp.int32)
    attended = jnp.zeros((TOKENS, HEADS * HEAD_DIM), jnp.bfloat16)
    cache_keys = jnp.zeros((CACHE_ROWS, KV_HEADS * HEAD_DIM), jnp.bfloat16)
    home_cache_values = jnp.zeros((CACHE_ROWS, KV_HEADS * HEAD_DIM), jnp.bfloat16)
    for prompt in range(PROMPTS):
        slot_ids = stretch_owner[prompt * MAX_STRETCHES:(prompt + 1) * MAX_STRETCHES].astype(jnp.int32)
        row_ids = (slot_ids[:, None] * STRETCH + jnp.arange(STRETCH, dtype=jnp.int32)[None, :]).reshape(-1)
        prompt_queries = queries[row_ids]
        prompt_keys = keys[row_ids]
        prompt_values = values[row_ids]
        live_rows = positions < lengths[prompt]
        visible = (positions[None, :] <= positions[:, None]) & live_rows[None, :]
        query_head_rows = prompt_queries.astype(jnp.float32).reshape(cache_span, HEADS, HEAD_DIM).transpose(1, 0, 2)
        key_heads = prompt_keys.astype(jnp.float32).reshape(cache_span, KV_HEADS, HEAD_DIM).transpose(1, 0, 2)
        value_heads = prompt_values.astype(jnp.float32).reshape(cache_span, KV_HEADS, HEAD_DIM).transpose(1, 0, 2)
        key_heads = jnp.repeat(key_heads, group_size, axis=0)
        value_heads = jnp.repeat(value_heads, group_size, axis=0)

        def one_head(operands):
            query_one, key_one, value_one = operands
            scores = jnp.einsum("id,jd->ij", query_one, key_one) * score_scale
            scores = jnp.where(visible, scores, -1e30)
            largest = jnp.max(scores, axis=-1, keepdims=True)
            weights = jnp.where(visible, jnp.exp(scores - largest), 0.0)
            totals = jnp.sum(weights, axis=-1, keepdims=True)
            rounded = lax.optimization_barrier(weights.astype(jnp.bfloat16)).astype(jnp.float32)
            return jnp.einsum("ij,jd->id", rounded, value_one) / totals

        outputs = lax.map(one_head, (query_head_rows, key_heads, value_heads))
        outputs = outputs.transpose(1, 0, 2).reshape(cache_span, HEADS * HEAD_DIM)
        outputs = outputs * live_rows[:, None].astype(jnp.float32)
        attended = attended.at[row_ids].set(outputs.astype(jnp.bfloat16))
        kept_keys = jnp.where(live_rows[:, None], prompt_keys, jnp.zeros_like(prompt_keys))
        kept_values = jnp.where(live_rows[:, None], prompt_values, jnp.zeros_like(prompt_values))
        start_row = (home_replica[prompt] * cache_span).astype(jnp.int32)
        zero_column = jnp.zeros((), jnp.int32)
        cache_keys = lax.dynamic_update_slice(cache_keys, kept_keys, (start_row, zero_column))
        home_cache_values = lax.dynamic_update_slice(home_cache_values, kept_values, (start_row, zero_column))
    group_cols = HEADS * HEAD_DIM // N_TP
    mixed_sum = jnp.zeros((TOKENS, D), jnp.float32)
    for group in range(N_TP):
        partial_value = jnp.dot(attended[:, group * group_cols:(group + 1) * group_cols], w_out[group * group_cols:(group + 1) * group_cols], preferred_element_type=jnp.float32)
        partial_value = lax.optimization_barrier(partial_value.astype(jnp.bfloat16)).astype(jnp.float32)
        mixed_sum = mixed_sum + partial_value
    mixed = mixed_sum.astype(jnp.bfloat16)
    return (mixed, cache_keys, home_cache_values)
```

```python
import functools

import jax
import jax.numpy as jnp
from jax import lax
from jax.experimental import pallas as pl
from jax.experimental.pallas import tpu as pltpu
from jax.sharding import PartitionSpec as P

HEAD_DIM = 128
MAX_STRETCHES = 8
CHUNKS = 4
LOG2_E = 1.4426950408889634
LOW = -1e30


def lookup(table, position):
    entries = jnp.arange(table.shape[0], dtype=jnp.int32)
    return jnp.sum(jnp.where(position[..., None] == entries, table, 0), axis=-1)


def attend_kernel(chunk, heads, info, q_ref, kv_hbm, w_hbm, out_ref, kv, w, q2, top, acc, att, kv_sem, w_sem):
    groups, rows = q_ref.shape[0], q_ref.shape[2]
    count = groups * rows
    stretch = kv.shape[1]
    mine, length = info[0], info[1]
    live = mine * stretch < length
    scale = HEAD_DIM ** (-0.5) * LOG2_E

    @pl.when(jnp.logical_not(live))
    def _():
        out_ref[...] = jnp.zeros_like(out_ref)

    @pl.when(live)
    def _():
        def fetch(i):
            return pltpu.make_async_copy(kv_hbm.at[info[2 + i]], kv.at[i, :, pl.ds(0, 2 * HEAD_DIM)], kv_sem.at[i])

        w_copy = pltpu.make_async_copy(w_hbm, w, w_sem)

        @pl.loop(0, mine + 1)
        def _(i):
            fetch(i).start()

        w_copy.start()
        for i in range(MAX_STRETCHES):
            kv[i, :, 2 * HEAD_DIM :] = jnp.ones((stretch, HEAD_DIM), jnp.bfloat16)
        for h in range(heads):
            q2[h * count : (h + 1) * count, :] = q_ref[:, 0, :, h * HEAD_DIM : (h + 1) * HEAD_DIM].reshape(
                count, HEAD_DIM
            )
        top[...] = jnp.full_like(top, LOW)
        acc[...] = jnp.zeros_like(acc)
        tile = 2 * count

        def block(i, diagonal):
            key = kv[i, :, 0:HEAD_DIM]
            value = kv[i, :, HEAD_DIM:]
            for t in range(heads * count // tile):
                part = slice(t * tile, (t + 1) * tile)
                scores = lax.dot_general(
                    q2[part, :], key, (((1,), (1,)), ((), ())), preferred_element_type=jnp.float32
                )
                if diagonal:
                    r = lax.broadcasted_iota(jnp.int32, (tile, stretch), 0) % count
                    at = r // rows * (CHUNKS * rows) + chunk * rows + r % rows
                    scores = jnp.where(lax.broadcasted_iota(jnp.int32, (tile, stretch), 1) <= at, scores, LOW)
                old = top[part, :]
                new = jnp.maximum(old, jnp.max(scores, axis=-1, keepdims=True) * scale)
                weights = jnp.exp2(scores * scale - jnp.concatenate([new] * (stretch // HEAD_DIM), axis=1))
                shrink = jnp.exp2(old - new)
                acc[part, :] = acc[part, :] * jnp.concatenate([shrink, shrink], axis=1) + jnp.dot(
                    weights.astype(jnp.bfloat16), value, preferred_element_type=jnp.float32
                )
                top[part, :] = new

        @pl.loop(0, mine)
        def _(i):
            fetch(i).wait()
            block(i, False)

        fetch(mine).wait()
        block(mine, True)

        r = lax.broadcasted_iota(jnp.int32, (count, HEAD_DIM), 0)
        at = mine * stretch + r // rows * (CHUNKS * rows) + chunk * rows + r % rows
        keep = (at < length).astype(jnp.float32)
        for h in range(heads):
            part = slice(h * count, (h + 1) * count)
            att[:, h * HEAD_DIM : (h + 1) * HEAD_DIM] = (
                acc[part, :HEAD_DIM] / acc[part, HEAD_DIM:] * keep
            ).astype(jnp.bfloat16)
        w_copy.wait()
        width = 1024
        for n in range(w.shape[1] // width):
            out_ref[:, n * width : (n + 1) * width] = jnp.dot(
                att[...], w[:, n * width : (n + 1) * width], preferred_element_type=jnp.float32
            ).astype(jnp.bfloat16)


def attend(chunk, info, queries, gathered, w_out):
    groups, _, rows, columns = queries.shape
    replicas, stretch, width = gathered.shape
    heads = columns // HEAD_DIM
    count = groups * rows
    features = w_out.shape[1]
    return pl.pallas_call(
        functools.partial(attend_kernel, chunk, heads),
        grid_spec=pltpu.PrefetchScalarGridSpec(
            num_scalar_prefetch=1,
            grid=(1,),
            in_specs=[
                pl.BlockSpec((groups, 1, rows, columns), lambda i, info: (0, chunk, 0, 0)),
                pl.BlockSpec(memory_space=pl.ANY),
                pl.BlockSpec(memory_space=pl.ANY),
            ],
            out_specs=pl.BlockSpec((count, features), lambda i, info: (0, 0)),
            scratch_shapes=[
                pltpu.VMEM((MAX_STRETCHES, stretch, width + HEAD_DIM), jnp.bfloat16),
                pltpu.VMEM(w_out.shape, jnp.bfloat16),
                pltpu.VMEM((heads * count, HEAD_DIM), jnp.bfloat16),
                pltpu.VMEM((heads * count, HEAD_DIM), jnp.float32),
                pltpu.VMEM((heads * count, 2 * HEAD_DIM), jnp.float32),
                pltpu.VMEM((count, columns), jnp.bfloat16),
                pltpu.SemaphoreType.DMA((MAX_STRETCHES,)),
                pltpu.SemaphoreType.DMA,
            ],
        ),
        out_shape=jax.ShapeDtypeStruct((count, features), jnp.bfloat16),
        compiler_params=pltpu.CompilerParams(vmem_limit_bytes=48 * 1024 * 1024),
        cost_estimate=pl.CostEstimate(
            flops=2 * count * columns * (features + 8 * stretch * 2), bytes_accessed=12 << 20, transcendentals=0
        ),
        name="attend_rows",
    )(info, queries, gathered, w_out)


def place_kernel(info, kv_ref, keys_ref, values_ref):
    stretch = kv_ref.shape[1]
    r = lax.broadcasted_iota(jnp.int32, (stretch, HEAD_DIM), 0)
    live = pl.program_id(0) * stretch + r < info[0]
    keys_ref[...] = jnp.where(live, kv_ref[0, :, :HEAD_DIM], 0)
    values_ref[...] = jnp.where(live, kv_ref[0, :, HEAD_DIM:], 0)


def place(info, gathered):
    replicas, stretch, width = gathered.shape
    cache = jax.ShapeDtypeStruct((MAX_STRETCHES * stretch, HEAD_DIM), jnp.bfloat16)
    return pl.pallas_call(
        place_kernel,
        grid_spec=pltpu.PrefetchScalarGridSpec(
            num_scalar_prefetch=1,
            grid=(MAX_STRETCHES,),
            in_specs=[pl.BlockSpec((1, stretch, width), lambda i, info: (info[1 + i], 0, 0))],
            out_specs=[pl.BlockSpec((stretch, HEAD_DIM), lambda i, info: (i, 0))] * 2,
        ),
        out_shape=[cache, cache],
        cost_estimate=pl.CostEstimate(flops=0, bytes_accessed=4 << 20, transcendentals=0),
        name="place_cache",
    )(info, gathered)


def shards(queries, keys, values, w_out, lengths, stretch_owner, home_replica):
    stretch = queries.shape[0]
    groups = lax.axis_size("tp")
    me = lax.axis_index("sp").astype(jnp.int32)
    slots = jnp.arange(stretch_owner.shape[0], dtype=jnp.int32)
    my_slot = jnp.sum(jnp.where(stretch_owner == me, slots, 0))
    prompt = my_slot // MAX_STRETCHES
    by_prompt = stretch_owner.reshape(-1, MAX_STRETCHES)
    prompts = jnp.arange(by_prompt.shape[0], dtype=jnp.int32)

    def owners(p):
        return jnp.sum(jnp.where((prompts == p)[:, None], by_prompt, 0), axis=0)

    info = jnp.concatenate([jnp.stack([my_slot % MAX_STRETCHES, lookup(lengths, prompt)]), owners(prompt)])
    homed = home_replica == me
    home_length = jnp.sum(jnp.where(homed, lengths, 0))
    home_prompt = jnp.sum(jnp.where(homed, prompts, 0))
    home_owners = jnp.where(jnp.any(homed), owners(home_prompt), 0)
    home_info = jnp.concatenate([home_length[None], home_owners])

    gathered = lax.all_gather(jnp.concatenate([keys, values], axis=1), "sp", axis=0)
    rows = stretch // groups // CHUNKS
    split = queries.reshape(groups, CHUNKS, rows, queries.shape[1])
    mixed = []
    for chunk in range(CHUNKS):
        partial = attend(chunk, info, split, gathered, w_out)
        mixed.append(lax.psum_scatter(partial, "tp", scatter_dimension=0, tiled=True))
    cache_keys, cache_values = place(home_info, gathered)
    return jnp.concatenate(mixed, axis=0), cache_keys, cache_values


def solution(mesh):
    placed = (P("sp", "tp"), P("sp", "tp"), P("sp", "tp"), P("tp", None), P(), P(), P())
    return jax.shard_map(
        shards,
        mesh=mesh,
        in_specs=placed,
        out_specs=(P(("sp", "tp"), None), P("sp", "tp"), P("sp", "tp")),
        check_vma=False,
    )
```

```python
import functools

import jax
import jax.numpy as jnp
from jax import lax
from jax.experimental import pallas as pl
from jax.experimental.pallas import tpu as pltpu
from jax.sharding import PartitionSpec as P

HEAD_DIM = 128
MAX_STRETCHES = 8
LOG2_E = 1.4426950408889634
LOW = -1e30


def lookup(table, position):
    entries = jnp.arange(table.shape[0], dtype=jnp.int32)
    return jnp.sum(jnp.where(position[..., None] == entries, table, 0), axis=-1)


def attend_kernel(heads, info, q_ref, kv_hbm, w_hbm, out_ref, kv, w, q2, top, acc, att, kv_sem, w_sem):
    count = q_ref.shape[0]
    stretch = kv.shape[1]
    mine, length = info[0], info[1]
    live = mine * stretch < length
    scale = HEAD_DIM ** (-0.5) * LOG2_E

    @pl.when(jnp.logical_not(live))
    def _():
        out_ref[...] = jnp.zeros_like(out_ref)

    @pl.when(live)
    def _():
        def fetch(i):
            return pltpu.make_async_copy(kv_hbm.at[info[2 + i]], kv.at[i, :, pl.ds(0, 2 * HEAD_DIM)], kv_sem.at[i])

        w_copy = pltpu.make_async_copy(w_hbm, w, w_sem)

        @pl.loop(0, mine + 1)
        def _(i):
            fetch(i).start()

        w_copy.start()
        for i in range(MAX_STRETCHES):
            kv[i, :, 2 * HEAD_DIM :] = jnp.ones((stretch, HEAD_DIM), jnp.bfloat16)
        for h in range(heads):
            q2[h * count : (h + 1) * count, :] = q_ref[:, h * HEAD_DIM : (h + 1) * HEAD_DIM]
        top[...] = jnp.full_like(top, LOW)
        acc[...] = jnp.zeros_like(acc)
        tile = min(256, count)

        def block(i, diagonal):
            for t in range(heads * count // tile):
                part = slice(t * tile, (t + 1) * tile)
                first = t * tile % count
                seen = first + tile if diagonal else stretch
                scores = lax.dot_general(
                    q2[part, :],
                    kv[i, :seen, :HEAD_DIM],
                    (((1,), (1,)), ((), ())),
                    preferred_element_type=jnp.float32,
                )
                if diagonal:
                    at = lax.broadcasted_iota(jnp.int32, (tile, seen), 0) + first
                    scores = jnp.where(lax.broadcasted_iota(jnp.int32, (tile, seen), 1) <= at, scores, LOW)
                old = top[part, :]
                new = jnp.maximum(old, jnp.max(scores, axis=-1, keepdims=True) * scale)
                weights = jnp.exp2(scores * scale - jnp.concatenate([new] * (seen // HEAD_DIM), axis=1))
                shrink = jnp.exp2(old - new)
                acc[part, :] = acc[part, :] * jnp.concatenate([shrink, shrink], axis=1) + jnp.dot(
                    weights.astype(jnp.bfloat16), kv[i, :seen, HEAD_DIM:], preferred_element_type=jnp.float32
                )
                top[part, :] = new

        @pl.loop(0, mine)
        def _(i):
            fetch(i).wait()
            block(i, False)

        fetch(mine).wait()
        block(mine, True)

        r = lax.broadcasted_iota(jnp.int32, (count, HEAD_DIM), 0)
        at = mine * stretch + r
        keep = (at < length).astype(jnp.float32)
        for h in range(heads):
            part = slice(h * count, (h + 1) * count)
            att[:, h * HEAD_DIM : (h + 1) * HEAD_DIM] = (
                acc[part, :HEAD_DIM] / acc[part, HEAD_DIM:] * keep
            ).astype(jnp.bfloat16)
        w_copy.wait()
        width = 1024
        for n in range(w.shape[1] // width):
            out_ref[:, n * width : (n + 1) * width] = jnp.dot(
                att[...], w[:, n * width : (n + 1) * width], preferred_element_type=jnp.float32
            ).astype(jnp.bfloat16)


def attend(info, queries, gathered, w_out):
    count, columns = queries.shape
    replicas, stretch, width = gathered.shape
    heads = columns // HEAD_DIM
    features = w_out.shape[1]
    return pl.pallas_call(
        functools.partial(attend_kernel, heads),
        grid_spec=pltpu.PrefetchScalarGridSpec(
            num_scalar_prefetch=1,
            grid=(1,),
            in_specs=[
                pl.BlockSpec((count, columns), lambda i, info: (0, 0)),
                pl.BlockSpec(memory_space=pl.ANY),
                pl.BlockSpec(memory_space=pl.ANY),
            ],
            out_specs=pl.BlockSpec((count, features), lambda i, info: (0, 0)),
            scratch_shapes=[
                pltpu.VMEM((MAX_STRETCHES, stretch, width + HEAD_DIM), jnp.bfloat16),
                pltpu.VMEM(w_out.shape, jnp.bfloat16),
                pltpu.VMEM((heads * count, HEAD_DIM), jnp.bfloat16),
                pltpu.VMEM((heads * count, HEAD_DIM), jnp.float32),
                pltpu.VMEM((heads * count, 2 * HEAD_DIM), jnp.float32),
                pltpu.VMEM((count, columns), jnp.bfloat16),
                pltpu.SemaphoreType.DMA((MAX_STRETCHES,)),
                pltpu.SemaphoreType.DMA,
            ],
        ),
        out_shape=jax.ShapeDtypeStruct((count, features), jnp.bfloat16),
        compiler_params=pltpu.CompilerParams(vmem_limit_bytes=48 * 1024 * 1024),
        cost_estimate=pl.CostEstimate(
            flops=2 * count * columns * (features + 8 * stretch * 2), bytes_accessed=12 << 20, transcendentals=0
        ),
        name="attend_rows",
    )(info, queries, gathered, w_out)


def place_kernel(info, kv_ref, keys_ref, values_ref):
    stretch = kv_ref.shape[1]
    r = lax.broadcasted_iota(jnp.int32, (stretch, HEAD_DIM), 0)
    live = pl.program_id(0) * stretch + r < info[0]
    keys_ref[...] = jnp.where(live, kv_ref[0, :, :HEAD_DIM], 0)
    values_ref[...] = jnp.where(live, kv_ref[0, :, HEAD_DIM:], 0)


def place(info, gathered):
    replicas, stretch, width = gathered.shape
    cache = jax.ShapeDtypeStruct((MAX_STRETCHES * stretch, HEAD_DIM), jnp.bfloat16)
    return pl.pallas_call(
        place_kernel,
        grid_spec=pltpu.PrefetchScalarGridSpec(
            num_scalar_prefetch=1,
            grid=(MAX_STRETCHES,),
            in_specs=[pl.BlockSpec((1, stretch, width), lambda i, info: (info[1 + i], 0, 0))],
            out_specs=[pl.BlockSpec((stretch, HEAD_DIM), lambda i, info: (i, 0))] * 2,
        ),
        out_shape=[cache, cache],
        cost_estimate=pl.CostEstimate(flops=0, bytes_accessed=4 << 20, transcendentals=0),
        name="place_cache",
    )(info, gathered)


def shards(queries, keys, values, w_out, lengths, stretch_owner, home_replica):
    me = lax.axis_index("sp").astype(jnp.int32)
    slots = jnp.arange(stretch_owner.shape[0], dtype=jnp.int32)
    my_slot = jnp.sum(jnp.where(stretch_owner == me, slots, 0))
    prompt = my_slot // MAX_STRETCHES
    by_prompt = stretch_owner.reshape(-1, MAX_STRETCHES)
    prompts = jnp.arange(by_prompt.shape[0], dtype=jnp.int32)

    def owners(p):
        return jnp.sum(jnp.where((prompts == p)[:, None], by_prompt, 0), axis=0)

    info = jnp.concatenate([jnp.stack([my_slot % MAX_STRETCHES, lookup(lengths, prompt)]), owners(prompt)])
    homed = home_replica == me
    home_length = jnp.sum(jnp.where(homed, lengths, 0))
    home_prompt = jnp.sum(jnp.where(homed, prompts, 0))
    home_owners = jnp.where(jnp.any(homed), owners(home_prompt), 0)
    home_info = jnp.concatenate([home_length[None], home_owners])

    gathered = lax.all_gather(jnp.concatenate([keys, values], axis=1), "sp", axis=0)
    partial = attend(info, queries, gathered, w_out)
    mixed = lax.psum_scatter(partial, "tp", scatter_dimension=0, tiled=True)
    cache_keys, cache_values = place(home_info, gathered)
    return mixed, cache_keys, cache_values


def solution(mesh):
    placed = (P("sp", "tp"), P("sp", "tp"), P("sp", "tp"), P("tp", None), P(), P(), P())
    return jax.shard_map(
        shards,
        mesh=mesh,
        in_specs=placed,
        out_specs=(P(("sp", "tp"), None), P("sp", "tp"), P("sp", "tp")),
        check_vma=False,
    )
```

```python
import functools

import jax
import jax.numpy as jnp
from jax import lax
from jax.experimental import pallas as pl
from jax.experimental.pallas import tpu as pltpu
from jax.sharding import PartitionSpec as P

HEAD_DIM = 128
MAX_STRETCHES = 8
SIDE = 4
LOG2_E = 1.4426950408889634
LOW = -1e30


def find(table, wanted, missing):
    return lax.fori_loop(
        0, table.shape[0], lambda j, found: jnp.where(table[j] == wanted, j, found), jnp.int32(missing)
    )


def held_at(me, owner):
    dx = lax.rem(owner // (2 * SIDE) - me // (2 * SIDE) + SIDE, SIDE)
    dy = lax.rem(lax.rem(owner // 2, SIDE) - lax.rem(me // 2, SIDE) + SIDE, SIDE)
    other = lax.rem(owner + me, 2)
    first = lax.rem(me, 2) == 0
    return jnp.where(first, dy, dx), jnp.where(first, dx, dy) * 2 + other


def start_half(pieces, piece, slot, target, sem):
    for p, ref in enumerate(pieces):

        @pl.when(piece == p)
        def _():
            pltpu.make_async_copy(ref.at[slot], target, sem).start()


def pick_kernel(home, me_ref, lengths, stretch_owner, home_replica, *refs):
    pieces, out, sem = refs[:SIDE], refs[SIDE], refs[SIDE + 1]
    me = me_ref[0]
    other = me + 1 - 2 * lax.rem(me, 2)
    if home:
        prompt = find(home_replica, other, 0)
    else:
        prompt = find(stretch_owner, other, 0) // MAX_STRETCHES
    for i in range(MAX_STRETCHES):
        piece, slot = held_at(me, stretch_owner[prompt * MAX_STRETCHES + i])
        start_half(pieces, piece, slot, out.at[i], sem.at[i])
    for i in range(MAX_STRETCHES):
        pltpu.make_async_copy(pieces[0].at[0], out.at[i], sem.at[i]).wait()


def pick(home, scalars, pieces):
    shape = (MAX_STRETCHES,) + pieces[0].shape[1:]
    return pl.pallas_call(
        functools.partial(pick_kernel, home),
        grid_spec=pltpu.PrefetchScalarGridSpec(
            num_scalar_prefetch=len(scalars),
            grid=(1,),
            in_specs=[pl.BlockSpec(memory_space=pl.ANY)] * SIDE,
            out_specs=pl.BlockSpec(memory_space=pl.ANY),
            scratch_shapes=[pltpu.SemaphoreType.DMA((MAX_STRETCHES,))],
        ),
        out_shape=jax.ShapeDtypeStruct(shape, jnp.bfloat16),
        compiler_params=pltpu.CompilerParams(vmem_limit_bytes=1024 * 1024),
        cost_estimate=pl.CostEstimate(flops=0, bytes_accessed=2 << 20, transcendentals=0),
        name="pick_home" if home else "pick_visible",
    )(*scalars, *pieces)


def attend_kernel(heads, me_ref, lengths, stretch_owner, home_replica, q_ref, *refs):
    pieces = refs[:SIDE]
    other_hbm, w_hbm, out_ref, kv, w, q2, top, acc, att, own_sem, other_sem, w_sem = refs[SIDE:]
    count = q_ref.shape[0]
    stretch = kv.shape[1]
    half = stretch // 2
    me = me_ref[0]
    slot = find(stretch_owner, me, 0)
    prompt = slot // MAX_STRETCHES
    mine = lax.rem(slot, MAX_STRETCHES)
    length = lengths[prompt]
    live = mine * stretch < length
    scale = HEAD_DIM ** (-0.5) * LOG2_E
    own_rows = pl.ds(pl.multiple_of(lax.rem(me, 2) * half, half), half)
    other_rows = pl.ds(pl.multiple_of((1 - lax.rem(me, 2)) * half, half), half)
    columns = pl.ds(0, 2 * HEAD_DIM)

    @pl.when(jnp.logical_not(live))
    def _():
        out_ref[...] = jnp.zeros_like(out_ref)

    @pl.when(live)
    def _():
        def other_copy(i):
            return pltpu.make_async_copy(other_hbm.at[i], kv.at[i, other_rows, columns], other_sem.at[i])

        def arrive(i):
            pltpu.make_async_copy(pieces[0].at[0], kv.at[i, own_rows, columns], own_sem.at[i]).wait()
            other_copy(i).wait()

        @pl.loop(0, mine + 1)
        def _(i):
            piece, at = held_at(me, stretch_owner[prompt * MAX_STRETCHES + i])
            start_half(pieces, piece, at, kv.at[i, own_rows, columns], own_sem.at[i])
            other_copy(i).start()

        w_copy = pltpu.make_async_copy(w_hbm, w, w_sem)
        w_copy.start()
        for i in range(MAX_STRETCHES):
            kv[i, :, 2 * HEAD_DIM :] = jnp.ones((stretch, HEAD_DIM), jnp.bfloat16)
        for h in range(heads):
            q2[h * count : (h + 1) * count, :] = q_ref[:, h * HEAD_DIM : (h + 1) * HEAD_DIM]
        top[...] = jnp.full_like(top, LOW)
        acc[...] = jnp.zeros_like(acc)
        tile = min(256, count)

        def block(i, diagonal):
            for t in range(heads * count // tile):
                part = slice(t * tile, (t + 1) * tile)
                first = t * tile % count
                seen = first + tile if diagonal else stretch
                scores = lax.dot_general(
                    q2[part, :],
                    kv[i, :seen, :HEAD_DIM],
                    (((1,), (1,)), ((), ())),
                    preferred_element_type=jnp.float32,
                )
                if diagonal:
                    at = lax.broadcasted_iota(jnp.int32, (tile, seen), 0) + first
                    scores = jnp.where(lax.broadcasted_iota(jnp.int32, (tile, seen), 1) <= at, scores, LOW)
                old = top[part, :]
                new = jnp.maximum(old, jnp.max(scores, axis=-1, keepdims=True) * scale)
                weights = jnp.exp2(scores * scale - jnp.concatenate([new] * (seen // HEAD_DIM), axis=1))
                shrink = jnp.exp2(old - new)
                acc[part, :] = acc[part, :] * jnp.concatenate([shrink, shrink], axis=1) + jnp.dot(
                    weights.astype(jnp.bfloat16), kv[i, :seen, HEAD_DIM:], preferred_element_type=jnp.float32
                )
                top[part, :] = new

        @pl.loop(0, mine)
        def _(i):
            arrive(i)
            block(i, False)

        arrive(mine)
        block(mine, True)

        at = mine * stretch + lax.broadcasted_iota(jnp.int32, (count, HEAD_DIM), 0)
        keep = (at < length).astype(jnp.float32)
        for h in range(heads):
            part = slice(h * count, (h + 1) * count)
            att[:, h * HEAD_DIM : (h + 1) * HEAD_DIM] = (
                acc[part, :HEAD_DIM] / acc[part, HEAD_DIM:] * keep
            ).astype(jnp.bfloat16)
        w_copy.wait()
        width = 1024
        for n in range(w.shape[1] // width):
            out_ref[:, n * width : (n + 1) * width] = jnp.dot(
                att[...], w[:, n * width : (n + 1) * width], preferred_element_type=jnp.float32
            ).astype(jnp.bfloat16)


def attend(scalars, queries, pieces, other, w_out):
    count, columns = queries.shape
    _, half, width = other.shape
    heads = columns // HEAD_DIM
    features = w_out.shape[1]
    return pl.pallas_call(
        functools.partial(attend_kernel, heads),
        grid_spec=pltpu.PrefetchScalarGridSpec(
            num_scalar_prefetch=len(scalars),
            grid=(1,),
            in_specs=[pl.BlockSpec((count, columns), lambda i, *_: (0, 0))]
            + [pl.BlockSpec(memory_space=pl.ANY)] * (SIDE + 2),
            out_specs=pl.BlockSpec((count, features), lambda i, *_: (0, 0)),
            scratch_shapes=[
                pltpu.VMEM((MAX_STRETCHES, 2 * half, width + HEAD_DIM), jnp.bfloat16),
                pltpu.VMEM(w_out.shape, jnp.bfloat16),
                pltpu.VMEM((heads * count, HEAD_DIM), jnp.bfloat16),
                pltpu.VMEM((heads * count, HEAD_DIM), jnp.float32),
                pltpu.VMEM((heads * count, 2 * HEAD_DIM), jnp.float32),
                pltpu.VMEM((count, columns), jnp.bfloat16),
                pltpu.SemaphoreType.DMA((MAX_STRETCHES,)),
                pltpu.SemaphoreType.DMA((MAX_STRETCHES,)),
                pltpu.SemaphoreType.DMA,
            ],
        ),
        out_shape=jax.ShapeDtypeStruct((count, features), jnp.bfloat16),
        compiler_params=pltpu.CompilerParams(vmem_limit_bytes=48 * 1024 * 1024),
        cost_estimate=pl.CostEstimate(
            flops=2 * count * columns * (features + 4 * MAX_STRETCHES * half), bytes_accessed=16 << 20, transcendentals=0
        ),
        name="attend_rows",
    )(*scalars, queries, *pieces, other, w_out)


def place_kernel(me_ref, lengths, stretch_owner, home_replica, *refs):
    pieces = refs[:SIDE]
    other_hbm, keys_ref, values_ref, kv, own_sem, other_sem = refs[SIDE:]
    stretch = kv.shape[1]
    half = stretch // 2
    me = me_ref[0]
    prompt = find(home_replica, me, -1)
    homed = prompt >= 0

    @pl.when(jnp.logical_not(homed))
    def _():
        keys_ref[...] = jnp.zeros_like(keys_ref)
        values_ref[...] = jnp.zeros_like(values_ref)

    @pl.when(homed)
    def _():
        own_rows = pl.ds(pl.multiple_of(lax.rem(me, 2) * half, half), half)
        other_rows = pl.ds(pl.multiple_of((1 - lax.rem(me, 2)) * half, half), half)
        length = lengths[prompt]
        for i in range(MAX_STRETCHES):
            piece, slot = held_at(me, stretch_owner[prompt * MAX_STRETCHES + i])
            start_half(pieces, piece, slot, kv.at[i, own_rows], own_sem.at[i])
            pltpu.make_async_copy(other_hbm.at[i], kv.at[i, other_rows], other_sem.at[i]).start()
        for i in range(MAX_STRETCHES):
            pltpu.make_async_copy(pieces[0].at[0], kv.at[i, own_rows], own_sem.at[i]).wait()
            pltpu.make_async_copy(other_hbm.at[i], kv.at[i, other_rows], other_sem.at[i]).wait()
            live = i * stretch + lax.broadcasted_iota(jnp.int32, (stretch, HEAD_DIM), 0) < length
            rows = slice(i * stretch, (i + 1) * stretch)
            keys_ref[rows, :] = jnp.where(live, kv[i, :, :HEAD_DIM], 0)
            values_ref[rows, :] = jnp.where(live, kv[i, :, HEAD_DIM:], 0)


def place(scalars, pieces, other):
    _, half, width = other.shape
    rows = MAX_STRETCHES * 2 * half
    cache = jax.ShapeDtypeStruct((rows, HEAD_DIM), jnp.bfloat16)
    return pl.pallas_call(
        place_kernel,
        grid_spec=pltpu.PrefetchScalarGridSpec(
            num_scalar_prefetch=len(scalars),
            grid=(1,),
            in_specs=[pl.BlockSpec(memory_space=pl.ANY)] * (SIDE + 1),
            out_specs=[pl.BlockSpec((rows, HEAD_DIM), lambda i, *_: (0, 0))] * 2,
            scratch_shapes=[
                pltpu.VMEM((MAX_STRETCHES, 2 * half, width), jnp.bfloat16),
                pltpu.SemaphoreType.DMA((MAX_STRETCHES,)),
                pltpu.SemaphoreType.DMA((MAX_STRETCHES,)),
            ],
        ),
        out_shape=[cache, cache],
        compiler_params=pltpu.CompilerParams(vmem_limit_bytes=8 * 1024 * 1024),
        cost_estimate=pl.CostEstimate(flops=0, bytes_accessed=4 << 20, transcendentals=0),
        name="place_cache",
    )(*scalars, *pieces, other)


def route(first, step):
    pairs = []
    for x in range(SIDE):
        for y in range(SIDE):
            for core in range(2):
                along_x = (core == 0) == first
                sx, sy = ((x + step) % SIDE, y) if along_x else (x, (y + step) % SIDE)
                pairs.append(((sx * SIDE + sy) * 2 + core, (x * SIDE + y) * 2 + core))
    return pairs


def swap_cores(array):
    return lax.ppermute(array, "sp", [(r, r + 1 - 2 * (r % 2)) for r in range(2 * SIDE * SIDE)])


def gather_halves(keys, values):
    core = lax.axis_index("sp") % 2
    half = keys.shape[0] // 2
    both = jnp.concatenate([keys, values], axis=1)
    got = swap_cores(lax.dynamic_slice_in_dim(both, (1 - core) * half, half, 0))
    chip = jnp.stack([lax.dynamic_slice_in_dim(both, core * half, half, 0), got])
    line = jnp.concatenate([chip] + [lax.ppermute(chip, "sp", route(True, step)) for step in range(1, SIDE)], axis=0)
    return [line] + [lax.ppermute(line, "sp", route(False, step)) for step in range(1, SIDE)]


def shards(queries, keys, values, w_out, lengths, stretch_owner, home_replica):
    me = lax.axis_index("sp").astype(jnp.int32).reshape(1)
    scalars = (me, lengths, stretch_owner, home_replica)
    pieces = gather_halves(keys, values)
    other = swap_cores(pick(False, scalars, pieces))
    partial = attend(scalars, queries, pieces, other, w_out)
    mixed = lax.psum_scatter(partial, "tp", scatter_dimension=0, tiled=True)
    home_other = swap_cores(pick(True, scalars, pieces))
    cache_keys, cache_values = place(scalars, pieces, home_other)
    return mixed, cache_keys, cache_values


def solution(mesh):
    placed = (P("sp", "tp"), P("sp", "tp"), P("sp", "tp"), P("tp", None), P(), P(), P())
    return jax.shard_map(
        shards,
        mesh=mesh,
        in_specs=placed,
        out_specs=(P(("sp", "tp"), None), P("sp", "tp"), P("sp", "tp")),
        check_vma=False,
    )
```

```python
import functools

import jax
import jax.numpy as jnp
from jax import lax
from jax.experimental import pallas as pl
from jax.experimental.pallas import tpu as pltpu
from jax.sharding import PartitionSpec as P

HEAD_DIM = 128
MAX_STRETCHES = 8
SIDE = 4
LOG2_E = 1.4426950408889634
LOW = -1e30
HALVES = 2


class Table:
    def __init__(self, ref):
        prompts = (ref.shape[0] - 1) // (MAX_STRETCHES + 2)
        self.me = ref[0]
        self.length = lambda p: ref[1 + p]
        self.home = lambda p: ref[1 + prompts + p]
        self.owner = lambda j: ref[1 + 2 * prompts + j]
        self.prompts = prompts

    def slot_of(self, replica):
        return self.find(self.owner, self.prompts * MAX_STRETCHES, replica, 0)

    def homed_at(self, replica, missing):
        return self.find(self.home, self.prompts, replica, missing)

    def find(self, entry, count, wanted, missing):
        return lax.fori_loop(
            0, count, lambda j, found: jnp.where(entry(j) == wanted, j, found), jnp.int32(missing)
        )


def held_at(me, owner):
    dx = lax.rem(owner // (2 * SIDE) - me // (2 * SIDE) + SIDE, SIDE)
    dy = lax.rem(lax.rem(owner // 2, SIDE) - lax.rem(me // 2, SIDE) + SIDE, SIDE)
    other = lax.rem(owner + me, 2)
    first = lax.rem(me, 2) == 0
    return jnp.where(first, dy, dx), jnp.where(first, dx, dy) * 2 + other


def start_half(pieces, piece, slot, target, sem):
    for p, ref in enumerate(pieces):

        @pl.when(piece == p)
        def _():
            pltpu.make_async_copy(ref.at[slot], target, sem).start()


def pick_kernel(info, *refs):
    pieces, outs, sem = refs[:SIDE], refs[SIDE : SIDE + 2], refs[SIDE + 2]
    table = Table(info)
    me = table.me
    other = me + 1 - 2 * lax.rem(me, 2)
    prompts = table.slot_of(other) // MAX_STRETCHES, table.homed_at(other, 0)
    for n in range(2):
        for i in range(MAX_STRETCHES):
            piece, slot = held_at(me, table.owner(prompts[n] * MAX_STRETCHES + i))
            start_half(pieces, piece, slot, outs[n].at[i], sem.at[n, i])
    for n in range(2):
        for i in range(MAX_STRETCHES):
            pltpu.make_async_copy(pieces[0].at[0], outs[n].at[i], sem.at[n, i]).wait()


def pick(info, pieces):
    shape = jax.ShapeDtypeStruct((MAX_STRETCHES,) + pieces[0].shape[1:], jnp.bfloat16)
    return pl.pallas_call(
        pick_kernel,
        grid_spec=pltpu.PrefetchScalarGridSpec(
            num_scalar_prefetch=1,
            grid=(1,),
            in_specs=[pl.BlockSpec(memory_space=pl.ANY)] * SIDE,
            out_specs=[pl.BlockSpec(memory_space=pl.ANY)] * 2,
            scratch_shapes=[pltpu.SemaphoreType.DMA((2, MAX_STRETCHES))],
        ),
        out_shape=[shape, shape],
        compiler_params=pltpu.CompilerParams(vmem_limit_bytes=1024 * 1024),
        cost_estimate=pl.CostEstimate(flops=0, bytes_accessed=4 << 20, transcendentals=0),
        name="pick_halves",
    )(info, *pieces)


def attend_kernel(heads, info, q_hbm, *refs):
    pieces = refs[:SIDE]
    other_hbm, w_hbm = refs[SIDE : SIDE + 2]
    outs = refs[SIDE + 2 : SIDE + 2 + HALVES]
    kv, w, q2, top, acc, att, ready, own_sem, other_sem, q_sem, w_sem, out_sem = refs[SIDE + 2 + HALVES :]
    count = q_hbm.shape[0]
    stretch = kv.shape[1]
    half = stretch // 2
    table = Table(info)
    me = table.me
    slot = table.slot_of(me)
    prompt = slot // MAX_STRETCHES
    mine = lax.rem(slot, MAX_STRETCHES)
    length = table.length(prompt)
    live = mine * stretch < length
    scale = HEAD_DIM ** (-0.5) * LOG2_E
    own_rows = pl.ds(pl.multiple_of(lax.rem(me, 2) * half, half), half)
    other_rows = pl.ds(pl.multiple_of((1 - lax.rem(me, 2)) * half, half), half)
    columns = pl.ds(0, 2 * HEAD_DIM)
    width = ready.shape[2]
    tiles = w.shape[1] // width

    def out_copy(n):
        at = n * width
        part = outs[0].shape[1]
        return pltpu.make_async_copy(
            ready.at[n % 2], outs[at // part].at[:, pl.ds(at % part, width)], out_sem.at[n % 2]
        )

    @pl.when(jnp.logical_not(live))
    def _():
        ready[...] = jnp.zeros_like(ready)
        for n in range(tiles):
            if n >= 2:
                out_copy(n - 2).wait()
            out_copy(n).start()

    @pl.when(live)
    def _():
        def q_copy(h):
            return pltpu.make_async_copy(
                q_hbm.at[:, pl.ds(h * HEAD_DIM, HEAD_DIM)], q2.at[pl.ds(h * count, count), :], q_sem.at[h]
            )

        def other_copy(i):
            return pltpu.make_async_copy(other_hbm.at[i], kv.at[i, other_rows, columns], other_sem.at[i])

        def arrive(i):
            pltpu.make_async_copy(pieces[0].at[0], kv.at[i, own_rows, columns], own_sem.at[i]).wait()
            other_copy(i).wait()

        @pl.loop(0, mine + 1)
        def _(i):
            piece, at = held_at(me, table.owner(prompt * MAX_STRETCHES + i))
            start_half(pieces, piece, at, kv.at[i, own_rows, columns], own_sem.at[i])
            other_copy(i).start()

        for h in range(heads):
            q_copy(h).start()
        w_copy = pltpu.make_async_copy(w_hbm, w, w_sem)
        w_copy.start()
        for i in range(MAX_STRETCHES):
            kv[i, :, 2 * HEAD_DIM :] = jnp.ones((stretch, HEAD_DIM), jnp.bfloat16)
        top[...] = jnp.full_like(top, LOW)
        acc[...] = jnp.zeros_like(acc)
        for h in range(heads):
            q_copy(h).wait()
        tile = min(256, count)

        def block(i, diagonal):
            for t in range(heads * count // tile):
                part = slice(t * tile, (t + 1) * tile)
                first = t * tile % count
                seen = first + tile if diagonal else stretch
                scores = lax.dot_general(
                    q2[part, :],
                    kv[i, :seen, :HEAD_DIM],
                    (((1,), (1,)), ((), ())),
                    preferred_element_type=jnp.float32,
                )
                if diagonal:
                    at = lax.broadcasted_iota(jnp.int32, (tile, seen), 0) + first
                    scores = jnp.where(lax.broadcasted_iota(jnp.int32, (tile, seen), 1) <= at, scores, LOW)
                old = top[part, :]
                new = jnp.maximum(old, jnp.max(scores, axis=-1, keepdims=True) * scale)
                weights = jnp.exp2(scores * scale - jnp.concatenate([new] * (seen // HEAD_DIM), axis=1))
                shrink = jnp.exp2(old - new)
                acc[part, :] = acc[part, :] * jnp.concatenate([shrink, shrink], axis=1) + jnp.dot(
                    weights.astype(jnp.bfloat16), kv[i, :seen, HEAD_DIM:], preferred_element_type=jnp.float32
                )
                top[part, :] = new

        @pl.loop(0, mine)
        def _(i):
            arrive(i)
            block(i, False)

        arrive(mine)
        block(mine, True)

        at = mine * stretch + lax.broadcasted_iota(jnp.int32, (count, HEAD_DIM), 0)
        keep = (at < length).astype(jnp.float32)
        for h in range(heads):
            part = slice(h * count, (h + 1) * count)
            att[:, h * HEAD_DIM : (h + 1) * HEAD_DIM] = (
                acc[part, :HEAD_DIM] / acc[part, HEAD_DIM:] * keep
            ).astype(jnp.bfloat16)
        w_copy.wait()
        for n in range(tiles):
            if n >= 2:
                out_copy(n - 2).wait()
            ready[n % 2] = jnp.dot(
                att[...], w[:, n * width : (n + 1) * width], preferred_element_type=jnp.float32
            ).astype(jnp.bfloat16)
            out_copy(n).start()

    for n in range(tiles - 2, tiles):
        out_copy(n).wait()


def attend(info, queries, pieces, other, w_out):
    count, columns = queries.shape
    _, half, width = other.shape
    heads = columns // HEAD_DIM
    features = w_out.shape[1]
    return pl.pallas_call(
        functools.partial(attend_kernel, heads),
        grid_spec=pltpu.PrefetchScalarGridSpec(
            num_scalar_prefetch=1,
            grid=(1,),
            in_specs=[pl.BlockSpec(memory_space=pltpu.HBM)]
            + [pl.BlockSpec(memory_space=pl.ANY)] * (SIDE + 1)
            + [pl.BlockSpec(memory_space=pltpu.HBM)],
            out_specs=[pl.BlockSpec(memory_space=pltpu.HBM)] * HALVES,
            scratch_shapes=[
                pltpu.VMEM((MAX_STRETCHES, 2 * half, width + HEAD_DIM), jnp.bfloat16),
                pltpu.VMEM(w_out.shape, jnp.bfloat16),
                pltpu.VMEM((heads * count, HEAD_DIM), jnp.bfloat16),
                pltpu.VMEM((heads * count, HEAD_DIM), jnp.float32),
                pltpu.VMEM((heads * count, 2 * HEAD_DIM), jnp.float32),
                pltpu.VMEM((count, columns), jnp.bfloat16),
                pltpu.VMEM((2, count, 512), jnp.bfloat16),
                pltpu.SemaphoreType.DMA((MAX_STRETCHES,)),
                pltpu.SemaphoreType.DMA((MAX_STRETCHES,)),
                pltpu.SemaphoreType.DMA((heads,)),
                pltpu.SemaphoreType.DMA,
                pltpu.SemaphoreType.DMA((2,)),
            ],
        ),
        out_shape=[jax.ShapeDtypeStruct((count, features // HALVES), jnp.bfloat16)] * HALVES,
        compiler_params=pltpu.CompilerParams(vmem_limit_bytes=50 * 1024 * 1024),
        cost_estimate=pl.CostEstimate(
            flops=2 * count * columns * (features + 4 * MAX_STRETCHES * half), bytes_accessed=16 << 20, transcendentals=0
        ),
        name="attend_rows",
    )(info, queries, *pieces, other, w_out)


def place_kernel(info, *refs):
    pieces = refs[:SIDE]
    other_hbm, keys_ref, values_ref, kv, own_sem, other_sem = refs[SIDE:]
    stretch = kv.shape[1]
    half = stretch // 2
    table = Table(info)
    me = table.me
    prompt = table.homed_at(me, -1)
    homed = prompt >= 0

    @pl.when(jnp.logical_not(homed))
    def _():
        keys_ref[...] = jnp.zeros_like(keys_ref)
        values_ref[...] = jnp.zeros_like(values_ref)

    @pl.when(homed)
    def _():
        own_rows = pl.ds(pl.multiple_of(lax.rem(me, 2) * half, half), half)
        other_rows = pl.ds(pl.multiple_of((1 - lax.rem(me, 2)) * half, half), half)
        length = table.length(prompt)
        for i in range(MAX_STRETCHES):
            piece, slot = held_at(me, table.owner(prompt * MAX_STRETCHES + i))
            start_half(pieces, piece, slot, kv.at[i, own_rows], own_sem.at[i])
            pltpu.make_async_copy(other_hbm.at[i], kv.at[i, other_rows], other_sem.at[i]).start()
        for i in range(MAX_STRETCHES):
            pltpu.make_async_copy(pieces[0].at[0], kv.at[i, own_rows], own_sem.at[i]).wait()
            pltpu.make_async_copy(other_hbm.at[i], kv.at[i, other_rows], other_sem.at[i]).wait()
            live = i * stretch + lax.broadcasted_iota(jnp.int32, (stretch, HEAD_DIM), 0) < length
            rows = slice(i * stretch, (i + 1) * stretch)
            keys_ref[rows, :] = jnp.where(live, kv[i, :, :HEAD_DIM], 0)
            values_ref[rows, :] = jnp.where(live, kv[i, :, HEAD_DIM:], 0)


def place(info, pieces, other):
    _, half, width = other.shape
    rows = MAX_STRETCHES * 2 * half
    cache = jax.ShapeDtypeStruct((rows, HEAD_DIM), jnp.bfloat16)
    return pl.pallas_call(
        place_kernel,
        grid_spec=pltpu.PrefetchScalarGridSpec(
            num_scalar_prefetch=1,
            grid=(1,),
            in_specs=[pl.BlockSpec(memory_space=pl.ANY)] * (SIDE + 1),
            out_specs=[pl.BlockSpec((rows, HEAD_DIM), lambda i, *_: (0, 0))] * 2,
            scratch_shapes=[
                pltpu.VMEM((MAX_STRETCHES, 2 * half, width), jnp.bfloat16),
                pltpu.SemaphoreType.DMA((MAX_STRETCHES,)),
                pltpu.SemaphoreType.DMA((MAX_STRETCHES,)),
            ],
        ),
        out_shape=[cache, cache],
        compiler_params=pltpu.CompilerParams(vmem_limit_bytes=8 * 1024 * 1024),
        cost_estimate=pl.CostEstimate(flops=0, bytes_accessed=4 << 20, transcendentals=0),
        name="place_cache",
    )(info, *pieces, other)


def route(first, step):
    pairs = []
    for x in range(SIDE):
        for y in range(SIDE):
            for core in range(2):
                along_x = (core == 0) == first
                sx, sy = ((x + step) % SIDE, y) if along_x else (x, (y + step) % SIDE)
                pairs.append(((sx * SIDE + sy) * 2 + core, (x * SIDE + y) * 2 + core))
    return pairs


def swap_cores(array):
    return lax.ppermute(array, "sp", [(r, r + 1 - 2 * (r % 2)) for r in range(2 * SIDE * SIDE)])


def gather_halves(keys, values):
    core = lax.axis_index("sp") % 2
    half = keys.shape[0] // 2

    def part(n):
        return jnp.concatenate([lax.dynamic_slice_in_dim(a, n * half, half, 0) for a in (keys, values)], axis=1)

    got = swap_cores(part(1 - core))
    chip = jnp.stack([part(core), got])
    line = jnp.concatenate([chip] + [lax.ppermute(chip, "sp", route(True, step)) for step in range(1, SIDE)], axis=0)
    return [line] + [lax.ppermute(line, "sp", route(False, step)) for step in range(1, SIDE)]


def sum_route(sense, replicas, groups):
    pairs = []
    for r in range(replicas):
        step = sense if r % 2 == 0 else -sense
        pairs += [(r * groups + z, r * groups + (z + step) % groups) for z in range(groups)]
    return pairs


def sum_scattered(partial):
    replicas, groups = lax.axis_size("sp"), lax.axis_size("tp")
    z = lax.axis_index("tp")
    sense = 1 - 2 * (lax.axis_index("sp") % 2)
    blocks = partial.reshape(groups, -1, partial.shape[1])
    routes = [sum_route(s, replicas, groups) for s in (1, -1)]
    hops = groups // 2

    def block(d):
        return lax.dynamic_index_in_dim(blocks, (d + 2 * groups) % groups, 0, keepdims=False).astype(jnp.float32)

    def hop(walked, d, route):
        sent = block(d) if walked is None else block(d) + walked.astype(jnp.float32)
        return lax.ppermute(sent.astype(jnp.bfloat16), ("sp", "tp"), route)

    long = short = None
    for k in range(hops):
        long = hop(long, z + sense * (hops - k), routes[0])
        if k < hops - 1:
            short = hop(short, z - sense * (hops - 1 - k), routes[1])
            long, short = lax.optimization_barrier((long, short))
    return (block(z) + long.astype(jnp.float32) + short.astype(jnp.float32)).astype(jnp.bfloat16)


def shards(queries, keys, values, w_out, lengths, stretch_owner, home_replica):
    me = lax.axis_index("sp").astype(jnp.int32).reshape(1)
    info = jnp.concatenate([me, lengths, home_replica, stretch_owner])
    pieces = gather_halves(keys, values)
    visible, homed = pick(info, pieces)
    visible_other = swap_cores(visible)
    home_other = swap_cores(homed)
    partials = attend(info, queries, pieces, visible_other, w_out)
    mixed = jnp.concatenate([sum_scattered(p) for p in partials], axis=1)
    cache_keys, cache_values = place(info, pieces, home_other)
    return mixed, cache_keys, cache_values


def solution(mesh):
    placed = (P("sp", "tp"), P("sp", "tp"), P("sp", "tp"), P("tp", None), P(), P(), P())
    return jax.shard_map(
        shards,
        mesh=mesh,
        in_specs=placed,
        out_specs=(P(("sp", "tp"), None), P("sp", "tp"), P("sp", "tp")),
        check_vma=False,
    )
```

```python
import functools

import jax
import jax.numpy as jnp
from jax import lax
from jax.experimental import pallas as pl
from jax.experimental.pallas import tpu as pltpu
from jax.sharding import PartitionSpec as P

HEAD_DIM = 128
MAX_STRETCHES = 8
SIDE = 4
LOG2_E = 1.4426950408889634
LOW = -1e30
PARTS = 2
EARLY = (0, 1)


class Table:
    def __init__(self, ref):
        prompts = (ref.shape[0] - 1) // (MAX_STRETCHES + 2)
        self.me = ref[0]
        self.length = lambda p: ref[1 + p]
        self.home = lambda p: ref[1 + prompts + p]
        self.owner = lambda j: ref[1 + 2 * prompts + j]
        self.prompts = prompts

    def slot_of(self, replica):
        return self.find(self.owner, self.prompts * MAX_STRETCHES, replica, 0)

    def homed_at(self, replica, missing):
        return self.find(self.home, self.prompts, replica, missing)

    def find(self, entry, count, wanted, missing):
        return lax.fori_loop(
            0, count, lambda j, found: jnp.where(entry(j) == wanted, j, found), jnp.int32(missing)
        )


def held_at(me, owner):
    dx = lax.rem(owner // (2 * SIDE) - me // (2 * SIDE) + SIDE, SIDE)
    dy = lax.rem(lax.rem(owner // 2, SIDE) - lax.rem(me // 2, SIDE) + SIDE, SIDE)
    other = lax.rem(owner + me, 2)
    first = lax.rem(me, 2) == 0
    return jnp.where(first, dy, dx), jnp.where(first, dx, dy) * 2 + other


def start_half(pieces, piece, slot, target, sem):
    for p, ref in enumerate(pieces):

        @pl.when(piece == p)
        def _():
            pltpu.make_async_copy(ref.at[slot], target, sem).start()


def pick_kernel(info, *refs):
    pieces, outs, sem = refs[:SIDE], refs[SIDE : SIDE + 2], refs[SIDE + 2]
    table = Table(info)
    me = table.me
    other = me + 1 - 2 * lax.rem(me, 2)
    prompts = table.slot_of(other) // MAX_STRETCHES, table.homed_at(other, 0)
    for n in range(2):
        for i in range(MAX_STRETCHES):
            piece, slot = held_at(me, table.owner(prompts[n] * MAX_STRETCHES + i))
            start_half(pieces, piece, slot, outs[n].at[i], sem.at[n, i])
    for n in range(2):
        for i in range(MAX_STRETCHES):
            pltpu.make_async_copy(pieces[0].at[0], outs[n].at[i], sem.at[n, i]).wait()


def pick(info, pieces):
    shape = jax.ShapeDtypeStruct((MAX_STRETCHES,) + pieces[0].shape[1:], jnp.bfloat16)
    return pl.pallas_call(
        pick_kernel,
        grid_spec=pltpu.PrefetchScalarGridSpec(
            num_scalar_prefetch=1,
            grid=(1,),
            in_specs=[pl.BlockSpec(memory_space=pl.ANY)] * SIDE,
            out_specs=[pl.BlockSpec(memory_space=pl.ANY)] * 2,
            scratch_shapes=[pltpu.SemaphoreType.DMA((2, MAX_STRETCHES))],
        ),
        out_shape=[shape, shape],
        compiler_params=pltpu.CompilerParams(vmem_limit_bytes=1024 * 1024),
        cost_estimate=pl.CostEstimate(flops=0, bytes_accessed=4 << 20, transcendentals=0),
        name="pick_halves",
    )(info, *pieces)


def update(q2, top, acc, tile, key, value, visible=None):
    scale = HEAD_DIM ** (-0.5) * LOG2_E
    scores = lax.dot_general(
        q2[tile].reshape(-1, HEAD_DIM), key, (((1,), (1,)), ((), ())), preferred_element_type=jnp.float32
    )
    if visible is not None:
        scores = jnp.where(visible, scores, LOW)
    old = top[tile]
    new = jnp.maximum(old, jnp.max(scores, axis=-1, keepdims=True) * scale)
    weights = jnp.exp2(scores * scale - jnp.concatenate([new] * (key.shape[0] // HEAD_DIM), axis=1))
    shrink = jnp.exp2(old - new)
    acc[tile] = acc[tile] * jnp.concatenate([shrink, shrink], axis=1) + jnp.dot(
        weights.astype(jnp.bfloat16), value, preferred_element_type=jnp.float32
    )
    top[tile] = new


def update_all(q2, top, acc, kv, kv_sem, source, count):
    half = kv.shape[1] // 2

    def arrive(n):
        slot = lax.rem(n, 2) * half
        target = kv.at[n // 2, pl.ds(pl.multiple_of(slot, half), half), pl.ds(0, 2 * HEAD_DIM)]
        pltpu.make_async_copy(source, target, kv_sem.at[n]).wait()

    @pl.loop(0, count // 2)
    def _(j):
        arrive(2 * j)
        arrive(2 * j + 1)
        for tile in range(q2.shape[0]):
            update(q2, top, acc, tile, kv[j, :, :HEAD_DIM], kv[j, :, HEAD_DIM:])

    @pl.when(lax.rem(count, 2) == 1)
    def _():
        arrive(count - 1)
        last = count // 2
        for tile in range(q2.shape[0]):
            update(q2, top, acc, tile, kv[last, :half, :HEAD_DIM], kv[last, :half, HEAD_DIM:])


class Work:
    def __init__(self, info, stretch):
        self.table = Table(info)
        self.me = self.table.me
        slot = self.table.slot_of(self.me)
        self.prompt = slot // MAX_STRETCHES
        self.mine = lax.rem(slot, MAX_STRETCHES)
        self.length = self.table.length(self.prompt)
        self.live = self.mine * stretch < self.length

    def start_own(self, pieces, wanted, kv, kv_sem):
        half = kv.shape[1] // 2
        count = jnp.int32(0)
        for i in range(MAX_STRETCHES - 1):
            piece, slot = held_at(self.me, self.table.owner(self.prompt * MAX_STRETCHES + i))
            chosen = functools.reduce(jnp.logical_or, [piece == p for p in wanted])
            chosen = jnp.logical_and(chosen, i < self.mine)
            first = pl.multiple_of(lax.rem(count, 2) * half, half)
            target = kv.at[count // 2, pl.ds(first, half), pl.ds(0, 2 * HEAD_DIM)]
            for p in wanted:

                @pl.when(jnp.logical_and(chosen, piece == p))
                def _():
                    pltpu.make_async_copy(pieces[p].at[slot], target, kv_sem.at[count]).start()

            count = count + chosen.astype(jnp.int32)
        return count

    def start_other(self, other, kv, kv_sem, count):
        half = kv.shape[1] // 2
        for i in range(MAX_STRETCHES - 1):
            first = pl.multiple_of(lax.rem(count, 2) * half, half)
            target = kv.at[count // 2, pl.ds(first, half), pl.ds(0, 2 * HEAD_DIM)]

            @pl.when(i < self.mine)
            def _():
                pltpu.make_async_copy(other.at[i], target, kv_sem.at[count]).start()

            count = count + (i < self.mine).astype(jnp.int32)
        return count


def query_copy(q_hbm, part, head, target, sem):
    return pltpu.make_async_copy(q_hbm.at[:, part, :, pl.ds(head * HEAD_DIM, HEAD_DIM)], target, sem)


def early_kernel(info, q_hbm, keys_hbm, values_hbm, *refs):
    pieces = dict(zip(EARLY, refs))
    top_hbm, acc_hbm, q2, own, kv, top, acc, q_sem, own_sem, kv_sem, state_sem = refs[len(EARLY) :]
    tiles, groups, rows, _ = q2.shape
    heads = tiles // PARTS
    stretch = own.shape[0]
    work = Work(info, stretch)

    @pl.when(work.live)
    def _():
        mine = [
            pltpu.make_async_copy(keys_hbm, own.at[:, pl.ds(0, HEAD_DIM)], own_sem.at[0]),
            pltpu.make_async_copy(values_hbm, own.at[:, pl.ds(HEAD_DIM, HEAD_DIM)], own_sem.at[1]),
        ]
        for copy in mine:
            copy.start()
        asked = [query_copy(q_hbm, t // heads, t % heads, q2.at[t], q_sem.at[t]) for t in range(tiles)]
        for copy in asked:
            copy.start()
        count = work.start_own(pieces, EARLY, kv, kv_sem)
        ones = jnp.ones((stretch, HEAD_DIM), jnp.bfloat16)
        own[:, 2 * HEAD_DIM :] = ones
        for j in range(kv.shape[0]):
            kv[j, :, 2 * HEAD_DIM :] = ones
        top[...] = jnp.full_like(top, LOW)
        acc[...] = jnp.zeros_like(acc)
        for copy in mine + asked:
            copy.wait()
        shape = (groups * rows, stretch)
        r = lax.broadcasted_iota(jnp.int32, shape, 0)
        for t in range(tiles):
            at = r // rows * (PARTS * rows) + t // heads * rows + r % rows
            visible = lax.broadcasted_iota(jnp.int32, shape, 1) <= at
            update(q2, top, acc, t, own[:, :HEAD_DIM], own[:, HEAD_DIM:], visible)
        update_all(q2, top, acc, kv, kv_sem, pieces[EARLY[0]].at[0], count)
        saved = [
            pltpu.make_async_copy(top, top_hbm, state_sem.at[0]),
            pltpu.make_async_copy(acc, acc_hbm, state_sem.at[1]),
        ]
        for copy in saved:
            copy.start()
        for copy in saved:
            copy.wait()


def attend_early(info, queries, keys, values, pieces):
    groups, _, rows, columns = queries.shape
    stretch = keys.shape[0]
    tiles = PARTS * columns // HEAD_DIM
    state = [(tiles, groups * rows, HEAD_DIM), (tiles, groups * rows, 2 * HEAD_DIM)]
    return pl.pallas_call(
        early_kernel,
        grid_spec=pltpu.PrefetchScalarGridSpec(
            num_scalar_prefetch=1,
            grid=(1,),
            in_specs=[pl.BlockSpec(memory_space=pl.ANY)] * (3 + len(EARLY)),
            out_specs=[pl.BlockSpec(memory_space=pl.ANY)] * 2,
            scratch_shapes=[
                pltpu.VMEM((tiles, groups, rows, HEAD_DIM), jnp.bfloat16),
                pltpu.VMEM((stretch, 3 * HEAD_DIM), jnp.bfloat16),
                pltpu.VMEM((MAX_STRETCHES // 2, stretch, 3 * HEAD_DIM), jnp.bfloat16),
                pltpu.VMEM(state[0], jnp.float32),
                pltpu.VMEM(state[1], jnp.float32),
                pltpu.SemaphoreType.DMA((tiles,)),
                pltpu.SemaphoreType.DMA((2,)),
                pltpu.SemaphoreType.DMA((MAX_STRETCHES,)),
                pltpu.SemaphoreType.DMA((2,)),
            ],
        ),
        out_shape=[jax.ShapeDtypeStruct(shape, jnp.float32) for shape in state],
        compiler_params=pltpu.CompilerParams(vmem_limit_bytes=48 * 1024 * 1024),
        cost_estimate=pl.CostEstimate(flops=6 << 30, bytes_accessed=10 << 20, transcendentals=0),
        name="attend_early",
    )(info, queries, keys, values, *[pieces[p] for p in EARLY])


def attend_kernel(part, info, q_hbm, *refs):
    late = [p for p in range(SIDE) if p not in EARLY]
    pieces = dict(zip(late, refs))
    refs = refs[len(late) :]
    other_hbm, top_hbm, acc_hbm, w_hbm, out, kv, w, q2, top, acc, att, ready = refs[:12]
    q_sem, kv_sem, state_sem, w_sem, out_sem = refs[12:]
    heads, groups, rows, _ = q2.shape
    stretch = kv.shape[1]
    work = Work(info, stretch)
    width = ready.shape[2]
    widths = w.shape[1] // width

    def out_copy(n):
        return pltpu.make_async_copy(ready.at[n % 2], out.at[:, pl.ds(n * width, width)], out_sem.at[n % 2])

    @pl.when(jnp.logical_not(work.live))
    def _():
        ready[...] = jnp.zeros_like(ready)
        for n in range(widths):
            if n >= 2:
                out_copy(n - 2).wait()
            out_copy(n).start()

    @pl.when(work.live)
    def _():
        tiles = pl.ds(part * heads, heads)
        state = [
            pltpu.make_async_copy(top_hbm.at[tiles], top, state_sem.at[0]),
            pltpu.make_async_copy(acc_hbm.at[tiles], acc, state_sem.at[1]),
        ]
        asked = [query_copy(q_hbm, part, h, q2.at[h], q_sem.at[h]) for h in range(heads)]
        for copy in asked + state:
            copy.start()
        count = work.start_own(pieces, late, kv, kv_sem)
        count = work.start_other(other_hbm, kv, kv_sem, count)
        w_copy = pltpu.make_async_copy(w_hbm, w, w_sem)
        w_copy.start()
        for j in range(kv.shape[0]):
            kv[j, :, 2 * HEAD_DIM :] = jnp.ones((stretch, HEAD_DIM), jnp.bfloat16)
        for copy in asked + state:
            copy.wait()
        update_all(q2, top, acc, kv, kv_sem, other_hbm.at[0], count)
        r = lax.broadcasted_iota(jnp.int32, (groups * rows, HEAD_DIM), 0)
        at = work.mine * stretch + r // rows * (PARTS * rows) + part * rows + r % rows
        keep = (at < work.length).astype(jnp.float32)
        for h in range(heads):
            att[:, h * HEAD_DIM : (h + 1) * HEAD_DIM] = (
                acc[h, :, :HEAD_DIM] / acc[h, :, HEAD_DIM:] * keep
            ).astype(jnp.bfloat16)
        w_copy.wait()
        for n in range(widths):
            if n >= 2:
                out_copy(n - 2).wait()
            ready[n % 2] = jnp.dot(
                att[...], w[:, n * width : (n + 1) * width], preferred_element_type=jnp.float32
            ).astype(jnp.bfloat16)
            out_copy(n).start()

    for n in range(widths - 2, widths):
        out_copy(n).wait()


def attend(part, info, queries, pieces, other, state, w_out):
    groups, _, rows, columns = queries.shape
    _, half, _ = other.shape
    stretch = 2 * half
    heads = columns // HEAD_DIM
    count = groups * rows
    features = w_out.shape[1]
    late = [pieces[p] for p in range(SIDE) if p not in EARLY]
    return pl.pallas_call(
        functools.partial(attend_kernel, part),
        grid_spec=pltpu.PrefetchScalarGridSpec(
            num_scalar_prefetch=1,
            grid=(1,),
            in_specs=[pl.BlockSpec(memory_space=pl.ANY)] * (5 + len(late)),
            out_specs=pl.BlockSpec(memory_space=pl.ANY),
            scratch_shapes=[
                pltpu.VMEM((MAX_STRETCHES - 1, stretch, 3 * HEAD_DIM), jnp.bfloat16),
                pltpu.VMEM(w_out.shape, jnp.bfloat16),
                pltpu.VMEM((heads, groups, rows, HEAD_DIM), jnp.bfloat16),
                pltpu.VMEM((heads, count, HEAD_DIM), jnp.float32),
                pltpu.VMEM((heads, count, 2 * HEAD_DIM), jnp.float32),
                pltpu.VMEM((count, columns), jnp.bfloat16),
                pltpu.VMEM((2, count, 512), jnp.bfloat16),
                pltpu.SemaphoreType.DMA((heads,)),
                pltpu.SemaphoreType.DMA((2 * MAX_STRETCHES,)),
                pltpu.SemaphoreType.DMA((2,)),
                pltpu.SemaphoreType.DMA,
                pltpu.SemaphoreType.DMA((2,)),
            ],
        ),
        out_shape=jax.ShapeDtypeStruct((count, features), jnp.bfloat16),
        compiler_params=pltpu.CompilerParams(vmem_limit_bytes=50 * 1024 * 1024),
        cost_estimate=pl.CostEstimate(
            flops=2 * count * columns * (features + 2 * MAX_STRETCHES * stretch), bytes_accessed=16 << 20, transcendentals=0
        ),
        name="attend_rows",
    )(info, queries, *late, other, *state, w_out)


def place_kernel(info, *refs):
    pieces = refs[:SIDE]
    other_hbm, keys_ref, values_ref, kv, own_sem, other_sem = refs[SIDE:]
    stretch = kv.shape[1]
    half = stretch // 2
    table = Table(info)
    me = table.me
    prompt = table.homed_at(me, -1)
    homed = prompt >= 0

    @pl.when(jnp.logical_not(homed))
    def _():
        keys_ref[...] = jnp.zeros_like(keys_ref)
        values_ref[...] = jnp.zeros_like(values_ref)

    @pl.when(homed)
    def _():
        own_rows = pl.ds(pl.multiple_of(lax.rem(me, 2) * half, half), half)
        other_rows = pl.ds(pl.multiple_of((1 - lax.rem(me, 2)) * half, half), half)
        length = table.length(prompt)
        for i in range(MAX_STRETCHES):
            piece, slot = held_at(me, table.owner(prompt * MAX_STRETCHES + i))
            start_half(pieces, piece, slot, kv.at[i, own_rows], own_sem.at[i])
            pltpu.make_async_copy(other_hbm.at[i], kv.at[i, other_rows], other_sem.at[i]).start()
        for i in range(MAX_STRETCHES):
            pltpu.make_async_copy(pieces[0].at[0], kv.at[i, own_rows], own_sem.at[i]).wait()
            pltpu.make_async_copy(other_hbm.at[i], kv.at[i, other_rows], other_sem.at[i]).wait()
            live = i * stretch + lax.broadcasted_iota(jnp.int32, (stretch, HEAD_DIM), 0) < length
            rows = slice(i * stretch, (i + 1) * stretch)
            keys_ref[rows, :] = jnp.where(live, kv[i, :, :HEAD_DIM], 0)
            values_ref[rows, :] = jnp.where(live, kv[i, :, HEAD_DIM:], 0)


def place(info, pieces, other):
    _, half, width = other.shape
    rows = MAX_STRETCHES * 2 * half
    cache = jax.ShapeDtypeStruct((rows, HEAD_DIM), jnp.bfloat16)
    return pl.pallas_call(
        place_kernel,
        grid_spec=pltpu.PrefetchScalarGridSpec(
            num_scalar_prefetch=1,
            grid=(1,),
            in_specs=[pl.BlockSpec(memory_space=pl.ANY)] * (SIDE + 1),
            out_specs=[pl.BlockSpec((rows, HEAD_DIM), lambda i, *_: (0, 0))] * 2,
            scratch_shapes=[
                pltpu.VMEM((MAX_STRETCHES, 2 * half, width), jnp.bfloat16),
                pltpu.SemaphoreType.DMA((MAX_STRETCHES,)),
                pltpu.SemaphoreType.DMA((MAX_STRETCHES,)),
            ],
        ),
        out_shape=[cache, cache],
        compiler_params=pltpu.CompilerParams(vmem_limit_bytes=8 * 1024 * 1024),
        cost_estimate=pl.CostEstimate(flops=0, bytes_accessed=4 << 20, transcendentals=0),
        name="place_cache",
    )(info, *pieces, other)


def route(first, step):
    pairs = []
    for x in range(SIDE):
        for y in range(SIDE):
            for core in range(2):
                along_x = (core == 0) == first
                sx, sy = ((x + step) % SIDE, y) if along_x else (x, (y + step) % SIDE)
                pairs.append(((sx * SIDE + sy) * 2 + core, (x * SIDE + y) * 2 + core))
    return pairs


def swap_cores(array):
    return lax.ppermute(array, "sp", [(r, r + 1 - 2 * (r % 2)) for r in range(2 * SIDE * SIDE)])


def gather_halves(keys, values):
    core = lax.axis_index("sp") % 2
    half = keys.shape[0] // 2

    def part(n):
        return jnp.concatenate([lax.dynamic_slice_in_dim(a, n * half, half, 0) for a in (keys, values)], axis=1)

    got = swap_cores(part(1 - core))
    chip = jnp.stack([part(core), got])
    line = jnp.concatenate([chip] + [lax.ppermute(chip, "sp", route(True, step)) for step in range(1, SIDE)], axis=0)
    return [line] + [lax.ppermute(line, "sp", route(False, step)) for step in range(1, SIDE)]


def sum_route(sense, replicas, groups):
    pairs = []
    for r in range(replicas):
        step = sense if r % 2 == 0 else -sense
        pairs += [(r * groups + z, r * groups + (z + step) % groups) for z in range(groups)]
    return pairs


def sum_scattered(partial):
    replicas, groups = lax.axis_size("sp"), lax.axis_size("tp")
    z = lax.axis_index("tp")
    sense = 1 - 2 * (lax.axis_index("sp") % 2)
    blocks = partial.reshape(groups, -1, partial.shape[1])
    routes = [sum_route(s, replicas, groups) for s in (1, -1)]
    hops = groups // 2

    def block(d):
        return lax.dynamic_index_in_dim(blocks, (d + 2 * groups) % groups, 0, keepdims=False).astype(jnp.float32)

    def hop(walked, d, route):
        sent = block(d) if walked is None else block(d) + walked.astype(jnp.float32)
        return lax.ppermute(sent.astype(jnp.bfloat16), ("sp", "tp"), route)

    long = short = None
    for k in range(hops):
        long = hop(long, z + sense * (hops - k), routes[0])
        if k < hops - 1:
            short = hop(short, z - sense * (hops - 1 - k), routes[1])
            long, short = lax.optimization_barrier((long, short))
    return (block(z) + long.astype(jnp.float32) + short.astype(jnp.float32)).astype(jnp.bfloat16)


def shards(queries, keys, values, w_out, lengths, stretch_owner, home_replica):
    me = lax.axis_index("sp").astype(jnp.int32).reshape(1)
    info = jnp.concatenate([me, lengths, home_replica, stretch_owner])
    groups = lax.axis_size("tp")
    split = queries.reshape(groups, PARTS, -1, queries.shape[1])
    pieces = gather_halves(keys, values)
    state = attend_early(info, split, keys, values, pieces)
    order, state = lax.optimization_barrier((info, state))
    visible, homed = pick(order, pieces)
    visible_other = swap_cores(visible)
    home_other = swap_cores(homed)
    mixed = jnp.concatenate(
        [sum_scattered(attend(p, info, split, pieces, visible_other, state, w_out)) for p in range(PARTS)], axis=0
    )
    cache_keys, cache_values = place(info, pieces, home_other)
    return mixed, cache_keys, cache_values


def solution(mesh):
    placed = (P("sp", "tp"), P("sp", "tp"), P("sp", "tp"), P("tp", None), P(), P(), P())
    return jax.shard_map(
        shards,
        mesh=mesh,
        in_specs=placed,
        out_specs=(P(("sp", "tp"), None), P("sp", "tp"), P("sp", "tp")),
        check_vma=False,
    )
```

```python
import functools

import jax
import jax.numpy as jnp
from jax import lax
from jax.experimental import pallas as pl
from jax.experimental.pallas import tpu as pltpu
from jax.sharding import PartitionSpec as P

HEAD_DIM = 128
MAX_STRETCHES = 8
SIDE = 4
LOG2_E = 1.4426950408889634
LOW = -1e30
TILE = 256
HALVES = 2
EARLY = (0, 1, 3)


class Table:
    def __init__(self, ref):
        prompts = (ref.shape[0] - 1) // (MAX_STRETCHES + 2)
        self.me = ref[0]
        self.length = lambda p: ref[1 + p]
        self.home = lambda p: ref[1 + prompts + p]
        self.owner = lambda j: ref[1 + 2 * prompts + j]
        self.prompts = prompts

    def slot_of(self, replica):
        return self.find(self.owner, self.prompts * MAX_STRETCHES, replica, 0)

    def homed_at(self, replica, missing):
        return self.find(self.home, self.prompts, replica, missing)

    def find(self, entry, count, wanted, missing):
        return lax.fori_loop(
            0, count, lambda j, found: jnp.where(entry(j) == wanted, j, found), jnp.int32(missing)
        )


def held_at(me, owner):
    bits = SIDE.bit_length() - 1
    dx = ((owner >> (bits + 1)) - (me >> (bits + 1))) & (SIDE - 1)
    dy = ((owner >> 1) - (me >> 1)) & (SIDE - 1)
    other = (owner ^ me) & 1
    first = (me & 1) == 0
    return jnp.where(first, dy, dx), jnp.where(first, dx, dy) * 2 + other


def start_half(pieces, piece, slot, target, sem):
    for p, ref in enumerate(pieces):

        @pl.when(piece == p)
        def _():
            pltpu.make_async_copy(ref.at[slot], target, sem).start()


def pick_kernel(info, *refs):
    pieces, outs, sem = refs[:SIDE], refs[SIDE : SIDE + 2], refs[SIDE + 2]
    table = Table(info)
    me = table.me
    other = me ^ 1
    prompts = table.slot_of(other) >> (MAX_STRETCHES.bit_length() - 1), table.homed_at(other, 0)
    for n in range(2):
        for i in range(MAX_STRETCHES):
            piece, slot = held_at(me, table.owner(prompts[n] * MAX_STRETCHES + i))
            start_half(pieces, piece, slot, outs[n].at[i], sem.at[n, i])
    for n in range(2):
        for i in range(MAX_STRETCHES):
            pltpu.make_async_copy(pieces[0].at[0], outs[n].at[i], sem.at[n, i]).wait()


def pick(info, pieces):
    shape = jax.ShapeDtypeStruct((MAX_STRETCHES,) + pieces[0].shape[1:], jnp.bfloat16)
    return pl.pallas_call(
        pick_kernel,
        grid_spec=pltpu.PrefetchScalarGridSpec(
            num_scalar_prefetch=1,
            grid=(1,),
            in_specs=[pl.BlockSpec(memory_space=pl.ANY)] * SIDE,
            out_specs=[pl.BlockSpec(memory_space=pl.ANY)] * 2,
            scratch_shapes=[pltpu.SemaphoreType.DMA((2, MAX_STRETCHES))],
        ),
        out_shape=[shape, shape],
        compiler_params=pltpu.CompilerParams(vmem_limit_bytes=1024 * 1024),
        cost_estimate=pl.CostEstimate(flops=0, bytes_accessed=4 << 20, transcendentals=0),
        name="pick_halves",
    )(info, *pieces)


def update(q2, top, acc, tile, key, value, visible=None):
    scale = HEAD_DIM ** (-0.5) * LOG2_E
    scores = lax.dot_general(
        q2[tile], key, (((1,), (1,)), ((), ())), preferred_element_type=jnp.float32
    )
    if visible is not None:
        scores = jnp.where(visible, scores, LOW)
    old = top[tile]
    new = jnp.maximum(old, jnp.max(scores, axis=-1, keepdims=True) * scale)
    weights = jnp.exp2(scores * scale - jnp.concatenate([new] * (key.shape[0] // HEAD_DIM), axis=1))
    shrink = jnp.exp2(old - new)
    acc[tile] = acc[tile] * jnp.concatenate([shrink, shrink], axis=1) + jnp.dot(
        weights.astype(jnp.bfloat16), value, preferred_element_type=jnp.float32
    )
    top[tile] = new


def update_all(q2, top, acc, kv, kv_sem, source, count):
    half = kv.shape[1] // 2

    def arrive(n):
        slot = (n & 1) * half
        target = kv.at[n >> 1, pl.ds(pl.multiple_of(slot, half), half), pl.ds(0, 2 * HEAD_DIM)]
        pltpu.make_async_copy(source, target, kv_sem.at[n]).wait()

    @pl.loop(0, count // 2)
    def _(j):
        arrive(2 * j)
        arrive(2 * j + 1)
        for tile in range(q2.shape[0]):
            update(q2, top, acc, tile, kv[j, :, :HEAD_DIM], kv[j, :, HEAD_DIM:])

    @pl.when((count & 1) == 1)
    def _():
        arrive(count - 1)
        last = count // 2
        for tile in range(q2.shape[0]):
            update(q2, top, acc, tile, kv[last, :half, :HEAD_DIM], kv[last, :half, HEAD_DIM:])


class Work:
    def __init__(self, info, stretch):
        self.table = Table(info)
        self.me = self.table.me
        slot = self.table.slot_of(self.me)
        self.prompt = slot >> (MAX_STRETCHES.bit_length() - 1)
        self.mine = slot & (MAX_STRETCHES - 1)
        self.length = self.table.length(self.prompt)
        self.live = self.mine * stretch < self.length

    def start_own(self, pieces, wanted, kv, kv_sem):
        half = kv.shape[1] // 2
        count = jnp.int32(0)
        for i in range(MAX_STRETCHES - 1):
            piece, slot = held_at(self.me, self.table.owner(self.prompt * MAX_STRETCHES + i))
            chosen = functools.reduce(jnp.logical_or, [piece == p for p in wanted])
            chosen = jnp.logical_and(chosen, i < self.mine)
            first = pl.multiple_of((count & 1) * half, half)
            target = kv.at[count >> 1, pl.ds(first, half), pl.ds(0, 2 * HEAD_DIM)]
            for p in wanted:

                @pl.when(jnp.logical_and(chosen, piece == p))
                def _():
                    pltpu.make_async_copy(pieces[p].at[slot], target, kv_sem.at[count]).start()

            count = count + chosen.astype(jnp.int32)
        return count

    def start_other(self, other, kv, kv_sem, count):
        half = kv.shape[1] // 2
        for i in range(MAX_STRETCHES - 1):
            first = pl.multiple_of((count & 1) * half, half)
            target = kv.at[count >> 1, pl.ds(first, half), pl.ds(0, 2 * HEAD_DIM)]

            @pl.when(i < self.mine)
            def _():
                pltpu.make_async_copy(other.at[i], target, kv_sem.at[count]).start()

            count = count + (i < self.mine).astype(jnp.int32)
        return count


def query_copies(q_hbm, q2, sem):
    rows = q2.shape[1]
    per_head = q_hbm.shape[0] // rows
    return [
        pltpu.make_async_copy(
            q_hbm.at[pl.ds(t % per_head * rows, rows), pl.ds(t // per_head * HEAD_DIM, HEAD_DIM)], q2.at[t], sem.at[t]
        )
        for t in range(q2.shape[0])
    ]


def early_kernel(info, q_hbm, keys_hbm, values_hbm, *refs):
    pieces = dict(zip(EARLY, refs))
    top_hbm, acc_hbm, q2, own, kv, top, acc, q_sem, own_sem, kv_sem, state_sem = refs[len(EARLY) :]
    tiles, rows, _ = q2.shape
    stretch = own.shape[0]
    work = Work(info, stretch)

    @pl.when(work.live)
    def _():
        mine = [
            pltpu.make_async_copy(keys_hbm, own.at[:, pl.ds(0, HEAD_DIM)], own_sem.at[0]),
            pltpu.make_async_copy(values_hbm, own.at[:, pl.ds(HEAD_DIM, HEAD_DIM)], own_sem.at[1]),
        ]
        for copy in mine:
            copy.start()
        asked = query_copies(q_hbm, q2, q_sem)
        for copy in asked:
            copy.start()
        count = work.start_own(pieces, EARLY, kv, kv_sem)
        ones = jnp.ones((stretch, HEAD_DIM), jnp.bfloat16)
        own[:, 2 * HEAD_DIM :] = ones
        for j in range(kv.shape[0]):
            kv[j, :, 2 * HEAD_DIM :] = ones
        top[...] = jnp.full_like(top, LOW)
        acc[...] = jnp.zeros_like(acc)
        for copy in mine + asked:
            copy.wait()
        for t in range(tiles):
            first = t * rows % stretch
            seen = first + rows
            at = first + lax.broadcasted_iota(jnp.int32, (rows, seen), 0)
            visible = lax.broadcasted_iota(jnp.int32, (rows, seen), 1) <= at
            update(q2, top, acc, t, own[:seen, :HEAD_DIM], own[:seen, HEAD_DIM:], visible)
        update_all(q2, top, acc, kv, kv_sem, pieces[EARLY[0]].at[0], count)
        saved = [
            pltpu.make_async_copy(top, top_hbm, state_sem.at[0]),
            pltpu.make_async_copy(acc, acc_hbm, state_sem.at[1]),
        ]
        for copy in saved:
            copy.start()
        for copy in saved:
            copy.wait()


def state_shapes(stretch, columns):
    tiles = stretch * columns // (TILE * HEAD_DIM)
    return [(tiles, TILE, HEAD_DIM), (tiles, TILE, 2 * HEAD_DIM)]


def attend_early(info, queries, keys, values, pieces):
    stretch, columns = queries.shape
    state = state_shapes(stretch, columns)
    tiles = state[0][0]
    return pl.pallas_call(
        early_kernel,
        grid_spec=pltpu.PrefetchScalarGridSpec(
            num_scalar_prefetch=1,
            grid=(1,),
            in_specs=[pl.BlockSpec(memory_space=pl.ANY)] * (3 + len(EARLY)),
            out_specs=[pl.BlockSpec(memory_space=pl.ANY)] * 2,
            scratch_shapes=[
                pltpu.VMEM(state[0], jnp.bfloat16),
                pltpu.VMEM((stretch, 3 * HEAD_DIM), jnp.bfloat16),
                pltpu.VMEM((MAX_STRETCHES // 2, stretch, 3 * HEAD_DIM), jnp.bfloat16),
                pltpu.VMEM(state[0], jnp.float32),
                pltpu.VMEM(state[1], jnp.float32),
                pltpu.SemaphoreType.DMA((tiles,)),
                pltpu.SemaphoreType.DMA((2,)),
                pltpu.SemaphoreType.DMA((MAX_STRETCHES,)),
                pltpu.SemaphoreType.DMA((2,)),
            ],
        ),
        out_shape=[jax.ShapeDtypeStruct(shape, jnp.float32) for shape in state],
        compiler_params=pltpu.CompilerParams(vmem_limit_bytes=48 * 1024 * 1024),
        cost_estimate=pl.CostEstimate(flops=6 << 30, bytes_accessed=10 << 20, transcendentals=0),
        name="attend_early",
    )(info, queries, keys, values, *[pieces[p] for p in EARLY])


def attend_kernel(info, q_hbm, *refs):
    late = [p for p in range(SIDE) if p not in EARLY]
    pieces = dict(zip(late, refs))
    refs = refs[len(late) :]
    other_hbm, top_hbm, acc_hbm, w_hbm = refs[:4]
    outs, refs = refs[4 : 4 + HALVES], refs[4 + HALVES :]
    kv, w, q2, top, acc, early_top, early_acc, att, ready = refs[:9]
    q_sem, kv_sem, state_sem, w_sem, out_sem = refs[9:]
    tiles, rows, _ = q2.shape
    stretch = kv.shape[1]
    work = Work(info, stretch)
    width = ready.shape[2]
    widths = w.shape[1] // width

    def out_copy(n):
        at = n * width
        part = outs[0].shape[1]
        return pltpu.make_async_copy(
            ready.at[n % 2], outs[at // part].at[:, pl.ds(at % part, width)], out_sem.at[n % 2]
        )

    @pl.when(jnp.logical_not(work.live))
    def _():
        ready[...] = jnp.zeros_like(ready)
        for n in range(widths):
            if n >= 2:
                out_copy(n - 2).wait()
            out_copy(n).start()

    @pl.when(work.live)
    def _():
        asked = query_copies(q_hbm, q2, q_sem)
        for copy in asked:
            copy.start()
        count = work.start_own(pieces, late, kv, kv_sem)
        count = work.start_other(other_hbm, kv, kv_sem, count)
        behind = [
            pltpu.make_async_copy(top_hbm, early_top, state_sem.at[0]),
            pltpu.make_async_copy(acc_hbm, early_acc, state_sem.at[1]),
            pltpu.make_async_copy(w_hbm, w, w_sem),
        ]
        for copy in behind:
            copy.start()
        for j in range(kv.shape[0]):
            kv[j, :, 2 * HEAD_DIM :] = jnp.ones((stretch, HEAD_DIM), jnp.bfloat16)
        top[...] = jnp.full_like(top, LOW)
        acc[...] = jnp.zeros_like(acc)
        for copy in asked:
            copy.wait()
        update_all(q2, top, acc, kv, kv_sem, other_hbm.at[0], count)
        for copy in behind:
            copy.wait()
        for t in range(tiles):
            first = t * rows % stretch
            at = work.mine * stretch + first + lax.broadcasted_iota(jnp.int32, (rows, HEAD_DIM), 0)
            keep = (at < work.length).astype(jnp.float32)
            most = jnp.maximum(top[t], early_top[t])
            one, two = jnp.exp2(top[t] - most), jnp.exp2(early_top[t] - most)
            sums = acc[t, :, :HEAD_DIM] * one + early_acc[t, :, :HEAD_DIM] * two
            totals = acc[t, :, HEAD_DIM:] * one + early_acc[t, :, HEAD_DIM:] * two
            column = t * rows // stretch * HEAD_DIM
            att[first : first + rows, column : column + HEAD_DIM] = (sums / totals * keep).astype(jnp.bfloat16)
        for n in range(widths):
            if n >= 2:
                out_copy(n - 2).wait()
            ready[n % 2] = jnp.dot(
                att[...], w[:, n * width : (n + 1) * width], preferred_element_type=jnp.float32
            ).astype(jnp.bfloat16)
            out_copy(n).start()

    for n in range(widths - 2, widths):
        out_copy(n).wait()


def attend(info, queries, pieces, other, state, w_out):
    stretch, columns = queries.shape
    features = w_out.shape[1]
    late = [pieces[p] for p in range(SIDE) if p not in EARLY]
    top, acc = state_shapes(stretch, columns)
    tiles = top[0]
    return pl.pallas_call(
        attend_kernel,
        grid_spec=pltpu.PrefetchScalarGridSpec(
            num_scalar_prefetch=1,
            grid=(1,),
            in_specs=[pl.BlockSpec(memory_space=pl.ANY)] * (5 + len(late)),
            out_specs=[pl.BlockSpec(memory_space=pl.ANY)] * HALVES,
            scratch_shapes=[
                pltpu.VMEM((MAX_STRETCHES - 1, stretch, 3 * HEAD_DIM), jnp.bfloat16),
                pltpu.VMEM(w_out.shape, jnp.bfloat16),
                pltpu.VMEM(top, jnp.bfloat16),
                pltpu.VMEM(top, jnp.float32),
                pltpu.VMEM(acc, jnp.float32),
                pltpu.VMEM(top, jnp.float32),
                pltpu.VMEM(acc, jnp.float32),
                pltpu.VMEM((stretch, columns), jnp.bfloat16),
                pltpu.VMEM((2, stretch, 512), jnp.bfloat16),
                pltpu.SemaphoreType.DMA((tiles,)),
                pltpu.SemaphoreType.DMA((2 * MAX_STRETCHES,)),
                pltpu.SemaphoreType.DMA((2,)),
                pltpu.SemaphoreType.DMA,
                pltpu.SemaphoreType.DMA((2,)),
            ],
        ),
        out_shape=[jax.ShapeDtypeStruct((stretch, features // HALVES), jnp.bfloat16)] * HALVES,
        compiler_params=pltpu.CompilerParams(vmem_limit_bytes=50 * 1024 * 1024),
        cost_estimate=pl.CostEstimate(
            flops=2 * stretch * columns * (features + 2 * MAX_STRETCHES * stretch), bytes_accessed=16 << 20, transcendentals=0
        ),
        name="attend_rows",
    )(info, queries, *late, other, *state, w_out)


def place_kernel(info, *refs):
    pieces = refs[:SIDE]
    other_hbm, keys_ref, values_ref, kv, own_sem, other_sem = refs[SIDE:]
    stretch = kv.shape[1]
    half = stretch // 2
    table = Table(info)
    me = table.me
    prompt = table.homed_at(me, -1)
    homed = prompt >= 0

    @pl.when(jnp.logical_not(homed))
    def _():
        keys_ref[...] = jnp.zeros_like(keys_ref)
        values_ref[...] = jnp.zeros_like(values_ref)

    @pl.when(homed)
    def _():
        own_rows = pl.ds(pl.multiple_of(lax.rem(me, 2) * half, half), half)
        other_rows = pl.ds(pl.multiple_of((1 - lax.rem(me, 2)) * half, half), half)
        length = table.length(prompt)
        for i in range(MAX_STRETCHES):
            piece, slot = held_at(me, table.owner(prompt * MAX_STRETCHES + i))
            start_half(pieces, piece, slot, kv.at[i, own_rows], own_sem.at[i])
            pltpu.make_async_copy(other_hbm.at[i], kv.at[i, other_rows], other_sem.at[i]).start()
        for i in range(MAX_STRETCHES):
            pltpu.make_async_copy(pieces[0].at[0], kv.at[i, own_rows], own_sem.at[i]).wait()
            pltpu.make_async_copy(other_hbm.at[i], kv.at[i, other_rows], other_sem.at[i]).wait()
            live = i * stretch + lax.broadcasted_iota(jnp.int32, (stretch, HEAD_DIM), 0) < length
            rows = slice(i * stretch, (i + 1) * stretch)
            keys_ref[rows, :] = jnp.where(live, kv[i, :, :HEAD_DIM], 0)
            values_ref[rows, :] = jnp.where(live, kv[i, :, HEAD_DIM:], 0)


def place(info, pieces, other):
    _, half, width = other.shape
    rows = MAX_STRETCHES * 2 * half
    cache = jax.ShapeDtypeStruct((rows, HEAD_DIM), jnp.bfloat16)
    return pl.pallas_call(
        place_kernel,
        grid_spec=pltpu.PrefetchScalarGridSpec(
            num_scalar_prefetch=1,
            grid=(1,),
            in_specs=[pl.BlockSpec(memory_space=pl.ANY)] * (SIDE + 1),
            out_specs=[pl.BlockSpec((rows, HEAD_DIM), lambda i, *_: (0, 0))] * 2,
            scratch_shapes=[
                pltpu.VMEM((MAX_STRETCHES, 2 * half, width), jnp.bfloat16),
                pltpu.SemaphoreType.DMA((MAX_STRETCHES,)),
                pltpu.SemaphoreType.DMA((MAX_STRETCHES,)),
            ],
        ),
        out_shape=[cache, cache],
        compiler_params=pltpu.CompilerParams(vmem_limit_bytes=8 * 1024 * 1024),
        cost_estimate=pl.CostEstimate(flops=0, bytes_accessed=4 << 20, transcendentals=0),
        name="place_cache",
    )(info, *pieces, other)


def route(first, step):
    pairs = []
    for x in range(SIDE):
        for y in range(SIDE):
            for core in range(2):
                along_x = (core == 0) == first
                sx, sy = ((x + step) % SIDE, y) if along_x else (x, (y + step) % SIDE)
                pairs.append(((sx * SIDE + sy) * 2 + core, (x * SIDE + y) * 2 + core))
    return pairs


def swap_cores(array):
    return lax.ppermute(array, "sp", [(r, r + 1 - 2 * (r % 2)) for r in range(2 * SIDE * SIDE)])


def gather_halves(keys, values):
    core = lax.axis_index("sp") % 2
    half = keys.shape[0] // 2

    def part(n):
        return jnp.concatenate([lax.dynamic_slice_in_dim(a, n * half, half, 0) for a in (keys, values)], axis=1)

    got = swap_cores(part(1 - core))
    chip = jnp.stack([part(core), got])
    line = jnp.concatenate([chip] + [lax.ppermute(chip, "sp", route(True, step)) for step in range(1, SIDE)], axis=0)
    near = {step: lax.ppermute(line, "sp", route(False, step)) for step in (1, SIDE - 1)}
    line, near = lax.optimization_barrier((line, near))
    far = {step: lax.ppermute(line, "sp", route(False, step)) for step in range(2, SIDE - 1)}
    return [line] + [{**near, **far}[step] for step in range(1, SIDE)]


def sum_route(sense, replicas, groups):
    pairs = []
    for r in range(replicas):
        step = sense if r % 2 == 0 else -sense
        pairs += [(r * groups + z, r * groups + (z + step) % groups) for z in range(groups)]
    return pairs


def sum_scattered(partial):
    replicas, groups = lax.axis_size("sp"), lax.axis_size("tp")
    z = lax.axis_index("tp")
    sense = 1 - 2 * (lax.axis_index("sp") % 2)
    blocks = partial.reshape(groups, -1, partial.shape[1])
    routes = [sum_route(s, replicas, groups) for s in (1, -1)]
    hops = groups // 2

    def block(d):
        return lax.dynamic_index_in_dim(blocks, (d + 2 * groups) % groups, 0, keepdims=False).astype(jnp.float32)

    def hop(walked, d, route):
        sent = block(d) if walked is None else block(d) + walked.astype(jnp.float32)
        return lax.ppermute(sent.astype(jnp.bfloat16), ("sp", "tp"), route)

    long = short = None
    for k in range(hops):
        long = hop(long, z + sense * (hops - k), routes[0])
        if k < hops - 1:
            short = hop(short, z - sense * (hops - 1 - k), routes[1])
            long, short = lax.optimization_barrier((long, short))
    return (block(z) + long.astype(jnp.float32) + short.astype(jnp.float32)).astype(jnp.bfloat16)


def shards(queries, keys, values, w_out, lengths, stretch_owner, home_replica):
    me = lax.axis_index("sp").astype(jnp.int32).reshape(1)
    info = jnp.concatenate([me, lengths, home_replica, stretch_owner])
    pieces = gather_halves(keys, values)
    state = attend_early(info, queries, keys, values, pieces)
    order, state = lax.optimization_barrier((info, state))
    visible, homed = pick(order, pieces)
    visible_other = swap_cores(visible)
    home_other = swap_cores(homed)
    partials = attend(info, queries, pieces, visible_other, state, w_out)
    mixed = jnp.concatenate([sum_scattered(p) for p in partials], axis=1)
    cache_keys, cache_values = place(info, pieces, home_other)
    return mixed, cache_keys, cache_values


def solution(mesh):
    placed = (P("sp", "tp"), P("sp", "tp"), P("sp", "tp"), P("tp", None), P(), P(), P())
    return jax.shard_map(
        shards,
        mesh=mesh,
        in_specs=placed,
        out_specs=(P(("sp", "tp"), None), P("sp", "tp"), P("sp", "tp")),
        check_vma=False,
    )
```

```python
import functools

import jax
import jax.numpy as jnp
from jax import lax
from jax.experimental import pallas as pl
from jax.experimental.pallas import tpu as pltpu
from jax.sharding import PartitionSpec as P

HEAD_DIM = 128
MAX_STRETCHES = 8
SIDE = 4
LOG2_E = 1.4426950408889634
LOW = -1e30
HALVES = 2


class Table:
    def __init__(self, ref):
        prompts = (ref.shape[0] - 2) // (MAX_STRETCHES + 2)
        self.me = ref[0]
        self.group = ref[1]
        self.length = lambda p: ref[2 + p]
        self.home = lambda p: ref[2 + prompts + p]
        self.owner = lambda j: ref[2 + 2 * prompts + j]
        self.prompts = prompts

    def slot_of(self, replica):
        return self.find(self.owner, self.prompts * MAX_STRETCHES, replica, 0)

    def homed_at(self, replica, missing):
        return self.find(self.home, self.prompts, replica, missing)

    def find(self, entry, count, wanted, missing):
        return lax.fori_loop(
            0, count, lambda j, found: jnp.where(entry(j) == wanted, j, found), jnp.int32(missing)
        )


def held_at(me, owner):
    bits = SIDE.bit_length() - 1
    dx = ((owner >> (bits + 1)) - (me >> (bits + 1))) & (SIDE - 1)
    dy = ((owner >> 1) - (me >> 1)) & (SIDE - 1)
    other = (owner ^ me) & 1
    first = (me & 1) == 0
    return jnp.where(first, dy, dx), jnp.where(first, dx, dy) * 2 + other


def start_half(pieces, piece, slot, target, sem):
    for p, ref in enumerate(pieces):

        @pl.when(piece == p)
        def _():
            pltpu.make_async_copy(ref.at[slot], target, sem).start()


def pick_kernel(home, info, *refs):
    pieces, out, sem = refs[:SIDE], refs[SIDE], refs[SIDE + 1]
    table = Table(info)
    me = table.me
    other = me ^ 1
    if home:
        prompt = table.homed_at(other, 0)
        count = jnp.int32(MAX_STRETCHES)
    else:
        slot = table.slot_of(other)
        prompt = slot >> (MAX_STRETCHES.bit_length() - 1)
        count = (slot & (MAX_STRETCHES - 1)) + 1

    @pl.loop(0, count)
    def _(i):
        piece, slot = held_at(me, table.owner(prompt * MAX_STRETCHES + i))
        start_half(pieces, piece, slot, out.at[i], sem.at[i])

    @pl.loop(0, count)
    def _(i):
        pltpu.make_async_copy(pieces[0].at[0], out.at[i], sem.at[i]).wait()


def pick(home, info, pieces):
    shape = jax.ShapeDtypeStruct((MAX_STRETCHES,) + pieces[0].shape[1:], jnp.bfloat16)
    return pl.pallas_call(
        functools.partial(pick_kernel, home),
        grid_spec=pltpu.PrefetchScalarGridSpec(
            num_scalar_prefetch=1,
            grid=(1,),
            in_specs=[pl.BlockSpec(memory_space=pl.ANY)] * SIDE,
            out_specs=pl.BlockSpec(memory_space=pl.ANY),
            scratch_shapes=[pltpu.SemaphoreType.DMA((MAX_STRETCHES,))],
        ),
        out_shape=shape,
        compiler_params=pltpu.CompilerParams(vmem_limit_bytes=1024 * 1024),
        cost_estimate=pl.CostEstimate(flops=0, bytes_accessed=2 << 20, transcendentals=0),
        name="pick_home" if home else "pick_visible",
    )(info, *pieces)


def attend_kernel(heads, groups, info, q_hbm, *refs):
    pieces = refs[:SIDE]
    other_hbm, w_hbm = refs[SIDE : SIDE + 2]
    outs = refs[SIDE + 2 : SIDE + 2 + HALVES * groups]
    kv, w, q2, top, acc, att, ready, own_sem, other_sem, q_sem, w_sem, out_sem = refs[SIDE + 2 + HALVES * groups :]
    count = q_hbm.shape[0]
    stretch = kv.shape[1]
    half = stretch // 2
    table = Table(info)
    me = table.me
    slot = table.slot_of(me)
    prompt = slot // MAX_STRETCHES
    mine = lax.rem(slot, MAX_STRETCHES)
    length = table.length(prompt)
    live = mine * stretch < length
    scale = HEAD_DIM ** (-0.5) * LOG2_E
    own_rows = pl.ds(pl.multiple_of(lax.rem(me, 2) * half, half), half)
    other_rows = pl.ds(pl.multiple_of((1 - lax.rem(me, 2)) * half, half), half)
    columns = pl.ds(0, 2 * HEAD_DIM)
    sense = 1 - 2 * (me & 1)
    rows = count // groups
    part_columns = outs[0].shape[1]

    def out_copy(half_index, n):
        target = (table.group + sense * walk(groups)[n]) & (groups - 1)
        source = ready.at[
            pl.ds(pl.multiple_of(target * rows, rows), rows), pl.ds(half_index * part_columns, part_columns)
        ]
        at = half_index * groups + n
        return pltpu.make_async_copy(source, outs[at], out_sem.at[at])

    @pl.when(jnp.logical_not(live))
    def _():
        ready[...] = jnp.zeros_like(ready)
        for half_index in range(HALVES):
            for n in range(groups):
                out_copy(half_index, n).start()

    @pl.when(live)
    def _():
        def q_copy(h):
            return pltpu.make_async_copy(
                q_hbm.at[:, pl.ds(h * HEAD_DIM, HEAD_DIM)], q2.at[pl.ds(h * count, count), :], q_sem.at[h]
            )

        def other_copy(i):
            return pltpu.make_async_copy(other_hbm.at[i], kv.at[i, other_rows, columns], other_sem.at[i])

        def arrive(i):
            pltpu.make_async_copy(pieces[0].at[0], kv.at[i, own_rows, columns], own_sem.at[i]).wait()
            other_copy(i).wait()

        @pl.loop(0, mine + 1)
        def _(i):
            piece, at = held_at(me, table.owner(prompt * MAX_STRETCHES + i))
            start_half(pieces, piece, at, kv.at[i, own_rows, columns], own_sem.at[i])
            other_copy(i).start()

        for h in range(heads):
            q_copy(h).start()
        w_copy = pltpu.make_async_copy(w_hbm, w, w_sem)
        w_copy.start()
        for i in range(MAX_STRETCHES):
            kv[i, :, 2 * HEAD_DIM :] = jnp.ones((stretch, HEAD_DIM), jnp.bfloat16)
        top[...] = jnp.full_like(top, LOW)
        acc[...] = jnp.zeros_like(acc)
        for h in range(heads):
            q_copy(h).wait()
        tile = min(256, count)

        def block(i, diagonal):
            for t in range(heads * count // tile):
                part = slice(t * tile, (t + 1) * tile)
                first = t * tile % count
                seen = first + tile if diagonal else stretch
                scores = lax.dot_general(
                    q2[part, :],
                    kv[i, :seen, :HEAD_DIM],
                    (((1,), (1,)), ((), ())),
                    preferred_element_type=jnp.float32,
                )
                if diagonal:
                    at = lax.broadcasted_iota(jnp.int32, (tile, seen), 0) + first
                    scores = jnp.where(lax.broadcasted_iota(jnp.int32, (tile, seen), 1) <= at, scores, LOW)
                old = top[part, :]
                new = jnp.maximum(old, jnp.max(scores, axis=-1, keepdims=True) * scale)
                weights = jnp.exp2(scores * scale - jnp.concatenate([new] * (seen // HEAD_DIM), axis=1))
                shrink = jnp.exp2(old - new)
                acc[part, :] = acc[part, :] * jnp.concatenate([shrink, shrink], axis=1) + jnp.dot(
                    weights.astype(jnp.bfloat16), kv[i, :seen, HEAD_DIM:], preferred_element_type=jnp.float32
                )
                top[part, :] = new

        @pl.loop(0, mine)
        def _(i):
            arrive(i)
            block(i, False)

        arrive(mine)
        block(mine, True)

        at = mine * stretch + lax.broadcasted_iota(jnp.int32, (count, HEAD_DIM), 0)
        keep = (at < length).astype(jnp.float32)
        for h in range(heads):
            part = slice(h * count, (h + 1) * count)
            att[:, h * HEAD_DIM : (h + 1) * HEAD_DIM] = (
                acc[part, :HEAD_DIM] / acc[part, HEAD_DIM:] * keep
            ).astype(jnp.bfloat16)
        w_copy.wait()
        width = 512
        for half_index in range(HALVES):
            for n in range(part_columns // width):
                columns_at = slice(half_index * part_columns + n * width, half_index * part_columns + (n + 1) * width)
                ready[:, columns_at] = jnp.dot(
                    att[...], w[:, columns_at], preferred_element_type=jnp.float32
                ).astype(jnp.bfloat16)
            for n in range(groups):
                out_copy(half_index, n).start()

    for half_index in range(HALVES):
        for n in range(groups):
            out_copy(half_index, n).wait()


def attend(info, queries, pieces, other, w_out, groups):
    count, columns = queries.shape
    _, half, width = other.shape
    heads = columns // HEAD_DIM
    features = w_out.shape[1]
    return pl.pallas_call(
        functools.partial(attend_kernel, heads, groups),
        grid_spec=pltpu.PrefetchScalarGridSpec(
            num_scalar_prefetch=1,
            grid=(1,),
            in_specs=[pl.BlockSpec(memory_space=pltpu.HBM)]
            + [pl.BlockSpec(memory_space=pl.ANY)] * (SIDE + 1)
            + [pl.BlockSpec(memory_space=pltpu.HBM)],
            out_specs=[pl.BlockSpec(memory_space=pl.ANY)] * (HALVES * groups),
            scratch_shapes=[
                pltpu.VMEM((MAX_STRETCHES, 2 * half, width + HEAD_DIM), jnp.bfloat16),
                pltpu.VMEM(w_out.shape, jnp.bfloat16),
                pltpu.VMEM((heads * count, HEAD_DIM), jnp.bfloat16),
                pltpu.VMEM((heads * count, HEAD_DIM), jnp.float32),
                pltpu.VMEM((heads * count, 2 * HEAD_DIM), jnp.float32),
                pltpu.VMEM((count, columns), jnp.bfloat16),
                pltpu.VMEM((count, features), jnp.bfloat16),
                pltpu.SemaphoreType.DMA((MAX_STRETCHES,)),
                pltpu.SemaphoreType.DMA((MAX_STRETCHES,)),
                pltpu.SemaphoreType.DMA((heads,)),
                pltpu.SemaphoreType.DMA,
                pltpu.SemaphoreType.DMA((HALVES * groups,)),
            ],
        ),
        out_shape=[jax.ShapeDtypeStruct((count // groups, features // HALVES), jnp.bfloat16)] * (HALVES * groups),
        compiler_params=pltpu.CompilerParams(vmem_limit_bytes=44 * 1024 * 1024),
        cost_estimate=pl.CostEstimate(
            flops=2 * count * columns * (features + 4 * MAX_STRETCHES * half), bytes_accessed=16 << 20, transcendentals=0
        ),
        name="attend_rows",
    )(info, queries, *pieces, other, w_out)


def place_kernel(info, *refs):
    pieces = refs[:SIDE]
    other_hbm, keys_ref, values_ref, kv, own_sem, other_sem = refs[SIDE:]
    stretch = kv.shape[1]
    half = stretch // 2
    table = Table(info)
    me = table.me
    prompt = table.homed_at(me, -1)
    homed = prompt >= 0

    @pl.when(jnp.logical_not(homed))
    def _():
        keys_ref[...] = jnp.zeros_like(keys_ref)
        values_ref[...] = jnp.zeros_like(values_ref)

    @pl.when(homed)
    def _():
        own_rows = pl.ds(pl.multiple_of(lax.rem(me, 2) * half, half), half)
        other_rows = pl.ds(pl.multiple_of((1 - lax.rem(me, 2)) * half, half), half)
        length = table.length(prompt)
        for i in range(MAX_STRETCHES):
            piece, slot = held_at(me, table.owner(prompt * MAX_STRETCHES + i))
            start_half(pieces, piece, slot, kv.at[i, own_rows], own_sem.at[i])
            pltpu.make_async_copy(other_hbm.at[i], kv.at[i, other_rows], other_sem.at[i]).start()
        for i in range(MAX_STRETCHES):
            pltpu.make_async_copy(pieces[0].at[0], kv.at[i, own_rows], own_sem.at[i]).wait()
            pltpu.make_async_copy(other_hbm.at[i], kv.at[i, other_rows], other_sem.at[i]).wait()
            live = i * stretch + lax.broadcasted_iota(jnp.int32, (stretch, HEAD_DIM), 0) < length
            rows = slice(i * stretch, (i + 1) * stretch)
            keys_ref[rows, :] = jnp.where(live, kv[i, :, :HEAD_DIM], 0)
            values_ref[rows, :] = jnp.where(live, kv[i, :, HEAD_DIM:], 0)


def place(info, pieces, other):
    _, half, width = other.shape
    rows = MAX_STRETCHES * 2 * half
    cache = jax.ShapeDtypeStruct((rows, HEAD_DIM), jnp.bfloat16)
    return pl.pallas_call(
        place_kernel,
        grid_spec=pltpu.PrefetchScalarGridSpec(
            num_scalar_prefetch=1,
            grid=(1,),
            in_specs=[pl.BlockSpec(memory_space=pl.ANY)] * (SIDE + 1),
            out_specs=[pl.BlockSpec((rows, HEAD_DIM), lambda i, *_: (0, 0))] * 2,
            scratch_shapes=[
                pltpu.VMEM((MAX_STRETCHES, 2 * half, width), jnp.bfloat16),
                pltpu.SemaphoreType.DMA((MAX_STRETCHES,)),
                pltpu.SemaphoreType.DMA((MAX_STRETCHES,)),
            ],
        ),
        out_shape=[cache, cache],
        compiler_params=pltpu.CompilerParams(vmem_limit_bytes=8 * 1024 * 1024),
        cost_estimate=pl.CostEstimate(flops=0, bytes_accessed=4 << 20, transcendentals=0),
        name="place_cache",
    )(info, *pieces, other)


def route(first, step):
    pairs = []
    for x in range(SIDE):
        for y in range(SIDE):
            for core in range(2):
                along_x = (core == 0) == first
                sx, sy = ((x + step) % SIDE, y) if along_x else (x, (y + step) % SIDE)
                pairs.append(((sx * SIDE + sy) * 2 + core, (x * SIDE + y) * 2 + core))
    return pairs


def swap_cores(array):
    return lax.ppermute(array, "sp", [(r, r + 1 - 2 * (r % 2)) for r in range(2 * SIDE * SIDE)])


def gather_halves(keys, values):
    core = lax.axis_index("sp") % 2
    half = keys.shape[0] // 2

    def part(n):
        return jnp.concatenate([lax.dynamic_slice_in_dim(a, n * half, half, 0) for a in (keys, values)], axis=1)

    got = swap_cores(part(1 - core))
    chip = jnp.stack([part(core), got])
    line = jnp.concatenate([chip] + [lax.ppermute(chip, "sp", route(True, step)) for step in range(1, SIDE)], axis=0)
    return [line] + [lax.ppermute(line, "sp", route(False, step)) for step in range(1, SIDE)]


def sum_route(sense, replicas, groups):
    pairs = []
    for r in range(replicas):
        step = sense if r % 2 == 0 else -sense
        pairs += [(r * groups + z, r * groups + (z + step) % groups) for z in range(groups)]
    return pairs


def walk(groups):
    hops = groups // 2
    return list(range(hops, 0, -1)) + list(range(1 - hops, 0)) + [0]


def sum_scattered(blocks):
    replicas, groups = lax.axis_size("sp"), lax.axis_size("tp")
    routes = [sum_route(s, replicas, groups) for s in (1, -1)]
    hops = groups // 2

    def hop(walked, block, route):
        if walked is not None:
            block = (block.astype(jnp.float32) + walked.astype(jnp.float32)).astype(jnp.bfloat16)
        return lax.ppermute(block, ("sp", "tp"), route)

    long = short = None
    for k in range(hops):
        long = hop(long, blocks[k], routes[0])
        if k < hops - 1:
            short = hop(short, blocks[hops + k], routes[1])
            long, short = lax.optimization_barrier((long, short))
    mine = blocks[groups - 1].astype(jnp.float32)
    return (mine + long.astype(jnp.float32) + short.astype(jnp.float32)).astype(jnp.bfloat16)


def shards(queries, keys, values, w_out, lengths, stretch_owner, home_replica):
    me = lax.axis_index("sp").astype(jnp.int32).reshape(1)
    group = lax.axis_index("tp").astype(jnp.int32).reshape(1)
    groups = lax.axis_size("tp")
    info = jnp.concatenate([me, group, lengths, home_replica, stretch_owner])
    pieces = gather_halves(keys, values)
    visible_other = swap_cores(pick(False, info, pieces))
    blocks = attend(info, queries, pieces, visible_other, w_out, groups)
    later, blocks = lax.optimization_barrier((info, blocks))
    mixed = jnp.concatenate([sum_scattered(blocks[h * groups : (h + 1) * groups]) for h in range(HALVES)], axis=1)
    home_other = swap_cores(pick(True, later, pieces))
    cache_keys, cache_values = place(info, pieces, home_other)
    return mixed, cache_keys, cache_values


def solution(mesh):
    placed = (P("sp", "tp"), P("sp", "tp"), P("sp", "tp"), P("tp", None), P(), P(), P())
    return jax.shard_map(
        shards,
        mesh=mesh,
        in_specs=placed,
        out_specs=(P(("sp", "tp"), None), P("sp", "tp"), P("sp", "tp")),
        check_vma=False,
    )
```

```python
import functools

import jax
import jax.numpy as jnp
from jax import lax
from jax.experimental import pallas as pl
from jax.experimental.pallas import tpu as pltpu
from jax.sharding import PartitionSpec as P

HEAD_DIM = 128
MAX_STRETCHES = 8
SIDE = 4
LOG2_E = 1.4426950408889634
LOW = -1e30
SHARES = (3, 1)


class Table:
    def __init__(self, ref):
        prompts = (ref.shape[0] - 2) // (MAX_STRETCHES + 2)
        self.me = ref[0]
        self.group = ref[1]
        self.length = lambda p: ref[2 + p]
        self.home = lambda p: ref[2 + prompts + p]
        self.owner = lambda j: ref[2 + 2 * prompts + j]
        self.prompts = prompts

    def slot_of(self, replica):
        return self.find(self.owner, self.prompts * MAX_STRETCHES, replica, 0)

    def homed_at(self, replica, missing):
        return self.find(self.home, self.prompts, replica, missing)

    def find(self, entry, count, wanted, missing):
        return lax.fori_loop(
            0, count, lambda j, found: jnp.where(entry(j) == wanted, j, found), jnp.int32(missing)
        )


def held_at(me, owner):
    bits = SIDE.bit_length() - 1
    dx = ((owner >> (bits + 1)) - (me >> (bits + 1))) & (SIDE - 1)
    dy = ((owner >> 1) - (me >> 1)) & (SIDE - 1)
    other = (owner ^ me) & 1
    first = (me & 1) == 0
    return jnp.where(first, dy, dx), jnp.where(first, dx, dy) * 2 + other


def start_half(pieces, piece, slot, target, sem):
    for p, ref in enumerate(pieces):

        @pl.when(piece == p)
        def _():
            pltpu.make_async_copy(ref.at[slot], target, sem).start()


def pick_kernel(home, info, *refs):
    pieces, out, sem = refs[:SIDE], refs[SIDE], refs[SIDE + 1]
    table = Table(info)
    me = table.me
    other = me ^ 1
    if home:
        prompt = table.homed_at(other, 0)
        count = jnp.int32(MAX_STRETCHES)
    else:
        slot = table.slot_of(other)
        prompt = slot >> (MAX_STRETCHES.bit_length() - 1)
        count = (slot & (MAX_STRETCHES - 1)) + 1

    @pl.loop(0, count)
    def _(i):
        piece, slot = held_at(me, table.owner(prompt * MAX_STRETCHES + i))
        start_half(pieces, piece, slot, out.at[i], sem.at[i])

    @pl.loop(0, count)
    def _(i):
        pltpu.make_async_copy(pieces[0].at[0], out.at[i], sem.at[i]).wait()


def pick(home, info, pieces):
    shape = jax.ShapeDtypeStruct((MAX_STRETCHES,) + pieces[0].shape[1:], jnp.bfloat16)
    return pl.pallas_call(
        functools.partial(pick_kernel, home),
        grid_spec=pltpu.PrefetchScalarGridSpec(
            num_scalar_prefetch=1,
            grid=(1,),
            in_specs=[pl.BlockSpec(memory_space=pl.ANY)] * SIDE,
            out_specs=pl.BlockSpec(memory_space=pl.ANY),
            scratch_shapes=[pltpu.SemaphoreType.DMA((MAX_STRETCHES,))],
        ),
        out_shape=shape,
        compiler_params=pltpu.CompilerParams(vmem_limit_bytes=1024 * 1024),
        cost_estimate=pl.CostEstimate(flops=0, bytes_accessed=2 << 20, transcendentals=0),
        name="pick_home" if home else "pick_visible",
    )(info, *pieces)


def attend_kernel(before, rows, info, q_hbm, *refs):
    pieces = refs[:SIDE]
    other_hbm, w_hbm = refs[SIDE : SIDE + 2]
    groups, per_group, _ = q_hbm.shape
    outs = refs[SIDE + 2 : SIDE + 2 + groups]
    kv, w, q2, top, acc, att, ready, own_sem, other_sem, q_sem, w_sem, out_sem = refs[SIDE + 2 + groups :]
    heads = q2.shape[0]
    count = groups * rows
    stretch = kv.shape[1]
    half = stretch // 2
    table = Table(info)
    me = table.me
    slot = table.slot_of(me)
    prompt = slot // MAX_STRETCHES
    mine = lax.rem(slot, MAX_STRETCHES)
    length = table.length(prompt)
    live = mine * stretch < length
    scale = HEAD_DIM ** (-0.5) * LOG2_E
    own_rows = pl.ds(pl.multiple_of(lax.rem(me, 2) * half, half), half)
    other_rows = pl.ds(pl.multiple_of((1 - lax.rem(me, 2)) * half, half), half)
    columns = pl.ds(0, 2 * HEAD_DIM)
    sense = 1 - 2 * (me & 1)
    halves = 2
    part_columns = w.shape[1] // halves

    def out_copy(half_index, n):
        target = (table.group + sense * walk(groups)[n]) & (groups - 1)
        columns_at = pl.ds(half_index * part_columns, part_columns)
        source = ready.at[pl.ds(pl.multiple_of(target * rows, rows), rows), columns_at]
        return pltpu.make_async_copy(source, outs[n].at[:, columns_at], out_sem.at[half_index * groups + n])

    @pl.when(jnp.logical_not(live))
    def _():
        ready[...] = jnp.zeros_like(ready)
        for half_index in range(halves):
            for n in range(groups):
                out_copy(half_index, n).start()

    @pl.when(live)
    def _():
        def q_copy(h):
            return pltpu.make_async_copy(
                q_hbm.at[:, pl.ds(before, rows), pl.ds(h * HEAD_DIM, HEAD_DIM)], q2.at[h], q_sem.at[h]
            )

        def other_copy(i):
            return pltpu.make_async_copy(other_hbm.at[i], kv.at[i, other_rows, columns], other_sem.at[i])

        def arrive(i):
            pltpu.make_async_copy(pieces[0].at[0], kv.at[i, own_rows, columns], own_sem.at[i]).wait()
            other_copy(i).wait()

        @pl.loop(0, mine + 1)
        def _(i):
            piece, at = held_at(me, table.owner(prompt * MAX_STRETCHES + i))
            start_half(pieces, piece, at, kv.at[i, own_rows, columns], own_sem.at[i])
            other_copy(i).start()

        for h in range(heads):
            q_copy(h).start()
        w_copy = pltpu.make_async_copy(w_hbm, w, w_sem)
        w_copy.start()
        for i in range(MAX_STRETCHES):
            kv[i, :, 2 * HEAD_DIM :] = jnp.ones((stretch, HEAD_DIM), jnp.bfloat16)
        top[...] = jnp.full_like(top, LOW)
        acc[...] = jnp.zeros_like(acc)
        for h in range(heads):
            q_copy(h).wait()
        together = max(1, 256 // count)
        tile = together * count

        def block(i, diagonal):
            for t in range(heads // together):
                part = slice(t * tile, (t + 1) * tile)
                scores = lax.dot_general(
                    q2[t * together : (t + 1) * together].reshape(tile, HEAD_DIM),
                    kv[i, :, :HEAD_DIM],
                    (((1,), (1,)), ((), ())),
                    preferred_element_type=jnp.float32,
                )
                if diagonal:
                    shape = (together, groups, rows, stretch)
                    at = lax.broadcasted_iota(jnp.int32, shape, 1) * per_group + before
                    at = at + lax.broadcasted_iota(jnp.int32, shape, 2)
                    visible = lax.broadcasted_iota(jnp.int32, shape, 3) <= at
                    scores = jnp.where(visible, scores.reshape(shape), LOW).reshape(tile, stretch)
                old = top[part, :]
                new = jnp.maximum(old, jnp.max(scores, axis=-1, keepdims=True) * scale)
                weights = jnp.exp2(scores * scale - jnp.concatenate([new] * (stretch // HEAD_DIM), axis=1))
                shrink = jnp.exp2(old - new)
                acc[part, :] = acc[part, :] * jnp.concatenate([shrink, shrink], axis=1) + jnp.dot(
                    weights.astype(jnp.bfloat16), kv[i, :, HEAD_DIM:], preferred_element_type=jnp.float32
                )
                top[part, :] = new

        @pl.loop(0, mine)
        def _(i):
            arrive(i)
            block(i, False)

        arrive(mine)
        block(mine, True)

        shape = (groups, rows, HEAD_DIM)
        at = lax.broadcasted_iota(jnp.int32, shape, 0) * per_group + lax.broadcasted_iota(jnp.int32, shape, 1)
        at = (at + (mine * stretch + before)).reshape(count, HEAD_DIM)
        keep = (at < length).astype(jnp.float32)
        for h in range(heads):
            part = slice(h * count, (h + 1) * count)
            att[:, h * HEAD_DIM : (h + 1) * HEAD_DIM] = (
                acc[part, :HEAD_DIM] / acc[part, HEAD_DIM:] * keep
            ).astype(jnp.bfloat16)
        w_copy.wait()
        width = 512
        for half_index in range(halves):
            for n in range(part_columns // width):
                columns_at = slice(half_index * part_columns + n * width, half_index * part_columns + (n + 1) * width)
                ready[:, columns_at] = jnp.dot(
                    att[...], w[:, columns_at], preferred_element_type=jnp.float32
                ).astype(jnp.bfloat16)
            for n in range(groups):
                out_copy(half_index, n).start()

    for half_index in range(halves):
        for n in range(groups):
            out_copy(half_index, n).wait()


def attend(before, rows, info, queries, pieces, other, w_out):
    groups, _, columns = queries.shape
    count = groups * rows
    _, half, width = other.shape
    heads = columns // HEAD_DIM
    features = w_out.shape[1]
    return pl.pallas_call(
        functools.partial(attend_kernel, before, rows),
        grid_spec=pltpu.PrefetchScalarGridSpec(
            num_scalar_prefetch=1,
            grid=(1,),
            in_specs=[pl.BlockSpec(memory_space=pltpu.HBM)]
            + [pl.BlockSpec(memory_space=pl.ANY)] * (SIDE + 1)
            + [pl.BlockSpec(memory_space=pltpu.HBM)],
            out_specs=[pl.BlockSpec(memory_space=pl.ANY)] * groups,
            scratch_shapes=[
                pltpu.VMEM((MAX_STRETCHES, 2 * half, width + HEAD_DIM), jnp.bfloat16),
                pltpu.VMEM(w_out.shape, jnp.bfloat16),
                pltpu.VMEM((heads, groups, rows, HEAD_DIM), jnp.bfloat16),
                pltpu.VMEM((heads * count, HEAD_DIM), jnp.float32),
                pltpu.VMEM((heads * count, 2 * HEAD_DIM), jnp.float32),
                pltpu.VMEM((count, columns), jnp.bfloat16),
                pltpu.VMEM((count, features), jnp.bfloat16),
                pltpu.SemaphoreType.DMA((MAX_STRETCHES,)),
                pltpu.SemaphoreType.DMA((MAX_STRETCHES,)),
                pltpu.SemaphoreType.DMA((heads,)),
                pltpu.SemaphoreType.DMA,
                pltpu.SemaphoreType.DMA((2 * groups,)),
            ],
        ),
        out_shape=[jax.ShapeDtypeStruct((rows, features), jnp.bfloat16)] * groups,
        compiler_params=pltpu.CompilerParams(vmem_limit_bytes=40 * 1024 * 1024),
        cost_estimate=pl.CostEstimate(
            flops=12 * count * columns * (features + 4 * MAX_STRETCHES * half), bytes_accessed=16 << 20, transcendentals=0
        ),
        name="attend_rows",
    )(info, queries, *pieces, other, w_out)


def place_kernel(info, *refs):
    pieces = refs[:SIDE]
    other_hbm, keys_ref, values_ref, kv, own_sem, other_sem = refs[SIDE:]
    stretch = kv.shape[1]
    half = stretch // 2
    table = Table(info)
    me = table.me
    prompt = table.homed_at(me, -1)
    homed = prompt >= 0

    @pl.when(jnp.logical_not(homed))
    def _():
        keys_ref[...] = jnp.zeros_like(keys_ref)
        values_ref[...] = jnp.zeros_like(values_ref)

    @pl.when(homed)
    def _():
        own_rows = pl.ds(pl.multiple_of(lax.rem(me, 2) * half, half), half)
        other_rows = pl.ds(pl.multiple_of((1 - lax.rem(me, 2)) * half, half), half)
        length = table.length(prompt)
        for i in range(MAX_STRETCHES):
            piece, slot = held_at(me, table.owner(prompt * MAX_STRETCHES + i))
            start_half(pieces, piece, slot, kv.at[i, own_rows], own_sem.at[i])
            pltpu.make_async_copy(other_hbm.at[i], kv.at[i, other_rows], other_sem.at[i]).start()
        for i in range(MAX_STRETCHES):
            pltpu.make_async_copy(pieces[0].at[0], kv.at[i, own_rows], own_sem.at[i]).wait()
            pltpu.make_async_copy(other_hbm.at[i], kv.at[i, other_rows], other_sem.at[i]).wait()
            live = i * stretch + lax.broadcasted_iota(jnp.int32, (stretch, HEAD_DIM), 0) < length
            rows = slice(i * stretch, (i + 1) * stretch)
            keys_ref[rows, :] = jnp.where(live, kv[i, :, :HEAD_DIM], 0)
            values_ref[rows, :] = jnp.where(live, kv[i, :, HEAD_DIM:], 0)


def place(info, pieces, other):
    _, half, width = other.shape
    rows = MAX_STRETCHES * 2 * half
    cache = jax.ShapeDtypeStruct((rows, HEAD_DIM), jnp.bfloat16)
    return pl.pallas_call(
        place_kernel,
        grid_spec=pltpu.PrefetchScalarGridSpec(
            num_scalar_prefetch=1,
            grid=(1,),
            in_specs=[pl.BlockSpec(memory_space=pl.ANY)] * (SIDE + 1),
            out_specs=[pl.BlockSpec((rows, HEAD_DIM), lambda i, *_: (0, 0))] * 2,
            scratch_shapes=[
                pltpu.VMEM((MAX_STRETCHES, 2 * half, width), jnp.bfloat16),
                pltpu.SemaphoreType.DMA((MAX_STRETCHES,)),
                pltpu.SemaphoreType.DMA((MAX_STRETCHES,)),
            ],
        ),
        out_shape=[cache, cache],
        compiler_params=pltpu.CompilerParams(vmem_limit_bytes=8 * 1024 * 1024),
        cost_estimate=pl.CostEstimate(flops=0, bytes_accessed=4 << 20, transcendentals=0),
        name="place_cache",
    )(info, *pieces, other)


def route(first, step):
    pairs = []
    for x in range(SIDE):
        for y in range(SIDE):
            for core in range(2):
                along_x = (core == 0) == first
                sx, sy = ((x + step) % SIDE, y) if along_x else (x, (y + step) % SIDE)
                pairs.append(((sx * SIDE + sy) * 2 + core, (x * SIDE + y) * 2 + core))
    return pairs


def swap_cores(array):
    return lax.ppermute(array, "sp", [(r, r + 1 - 2 * (r % 2)) for r in range(2 * SIDE * SIDE)])


def gather_halves(keys, values):
    core = lax.axis_index("sp") % 2
    half = keys.shape[0] // 2

    def part(n):
        return jnp.concatenate([lax.dynamic_slice_in_dim(a, n * half, half, 0) for a in (keys, values)], axis=1)

    got = swap_cores(part(1 - core))
    chip = jnp.stack([part(core), got])
    line = jnp.concatenate([chip] + [lax.ppermute(chip, "sp", route(True, step)) for step in range(1, SIDE)], axis=0)
    return [line] + [lax.ppermute(line, "sp", route(False, step)) for step in range(1, SIDE)]


def sum_route(sense, replicas, groups):
    pairs = []
    for r in range(replicas):
        step = sense if r % 2 == 0 else -sense
        pairs += [(r * groups + z, r * groups + (z + step) % groups) for z in range(groups)]
    return pairs


def walk(groups):
    hops = groups // 2
    return list(range(hops, 0, -1)) + list(range(1 - hops, 0)) + [0]


def hop(walked, block, sense):
    if walked is not None:
        block = (block.astype(jnp.float32) + walked.astype(jnp.float32)).astype(jnp.bfloat16)
    return lax.ppermute(block, ("sp", "tp"), sum_route(sense, lax.axis_size("sp"), lax.axis_size("tp")))


def first_hops(blocks):
    return hop(None, blocks[0], 1), hop(None, blocks[len(blocks) // 2], -1)


def sum_scattered(blocks, walks, done):
    hops = len(blocks) // 2
    long, short = walks
    for k in range(1, hops):
        long = hop(long, blocks[k], 1)
        if k < hops - 1:
            short = hop(short, blocks[hops + k], -1)
        if k < hops - 2:
            long, short = lax.optimization_barrier((long, short))
        elif k < hops - 1:
            long, short, done = lax.optimization_barrier((long, short, done))
    mine = blocks[-1].astype(jnp.float32)
    return (mine + long.astype(jnp.float32) + short.astype(jnp.float32)).astype(jnp.bfloat16), done


def shards(queries, keys, values, w_out, lengths, stretch_owner, home_replica):
    me = lax.axis_index("sp").astype(jnp.int32).reshape(1)
    group = lax.axis_index("tp").astype(jnp.int32).reshape(1)
    groups = lax.axis_size("tp")
    info = jnp.concatenate([me, group, lengths, home_replica, stretch_owner])
    pieces = gather_halves(keys, values)
    visible_other = swap_cores(pick(False, info, pieces))
    split = queries.reshape(groups, -1, queries.shape[1])
    unit = split.shape[1] // sum(SHARES)
    parts, walks, before, later = [], [], 0, info
    for share in SHARES:
        blocks = attend(before, share * unit, later, split, pieces, visible_other, w_out)
        later, blocks = lax.optimization_barrier((later, blocks))
        if walks:
            blocks, walks[-1] = lax.optimization_barrier((blocks, walks[-1]))
        parts.append(blocks)
        walks.append(first_hops(blocks))
        before += share * unit
    home_other = swap_cores(pick(True, later, pieces))
    caches = place(info, pieces, home_other)
    sums = []
    for blocks, walk_pair in zip(parts, walks):
        total, caches = sum_scattered(blocks, walk_pair, caches)
        sums.append(total)
    mixed = jnp.concatenate(sums, axis=0)
    cache_keys, cache_values = caches
    return mixed, cache_keys, cache_values


def solution(mesh):
    placed = (P("sp", "tp"), P("sp", "tp"), P("sp", "tp"), P("tp", None), P(), P(), P())
    return jax.shard_map(
        shards,
        mesh=mesh,
        in_specs=placed,
        out_specs=(P(("sp", "tp"), None), P("sp", "tp"), P("sp", "tp")),
        check_vma=False,
    )
```

```python
import functools

import jax
import jax.numpy as jnp
from jax import lax
from jax.experimental import pallas as pl
from jax.experimental.pallas import tpu as pltpu
from jax.sharding import PartitionSpec as P

HEAD_DIM = 128
MAX_STRETCHES = 8
SIDE = 4
LOG2_E = 1.4426950408889634
LOW = -1e30
HALVES = 2


class Table:
    def __init__(self, ref):
        prompts = (ref.shape[0] - 2) // (MAX_STRETCHES + 2)
        self.me = ref[0]
        self.group = ref[1]
        self.length = lambda p: ref[2 + p]
        self.home = lambda p: ref[2 + prompts + p]
        self.owner = lambda j: ref[2 + 2 * prompts + j]
        self.prompts = prompts

    def slot_of(self, replica):
        return self.find(self.owner, self.prompts * MAX_STRETCHES, replica, 0)

    def homed_at(self, replica, missing):
        return self.find(self.home, self.prompts, replica, missing)

    def find(self, entry, count, wanted, missing):
        return lax.fori_loop(
            0, count, lambda j, found: jnp.where(entry(j) == wanted, j, found), jnp.int32(missing)
        )


def held_at(me, owner):
    bits = SIDE.bit_length() - 1
    dx = ((owner >> (bits + 1)) - (me >> (bits + 1))) & (SIDE - 1)
    dy = ((owner >> 1) - (me >> 1)) & (SIDE - 1)
    other = (owner ^ me) & 1
    first = (me & 1) == 0
    return jnp.where(first, dy, dx), jnp.where(first, dx, dy) * 2 + other


def start_half(pieces, piece, slot, target, sem):
    for p, ref in enumerate(pieces):

        @pl.when(piece == p)
        def _():
            pltpu.make_async_copy(ref.at[slot], target, sem).start()


def pick_kernel(home, info, *refs):
    pieces, out, sem = refs[:SIDE], refs[SIDE], refs[SIDE + 1]
    table = Table(info)
    me = table.me
    other = me ^ 1
    if home:
        prompt = table.homed_at(other, 0)
        count = jnp.int32(MAX_STRETCHES)
    else:
        slot = table.slot_of(other)
        prompt = slot >> (MAX_STRETCHES.bit_length() - 1)
        count = (slot & (MAX_STRETCHES - 1)) + 1

    @pl.loop(0, count)
    def _(i):
        piece, slot = held_at(me, table.owner(prompt * MAX_STRETCHES + i))
        start_half(pieces, piece, slot, out.at[i], sem.at[i])

    @pl.loop(0, count)
    def _(i):
        pltpu.make_async_copy(pieces[0].at[0], out.at[i], sem.at[i]).wait()


def pick(home, info, pieces):
    shape = jax.ShapeDtypeStruct((MAX_STRETCHES,) + pieces[0].shape[1:], jnp.bfloat16)
    return pl.pallas_call(
        functools.partial(pick_kernel, home),
        grid_spec=pltpu.PrefetchScalarGridSpec(
            num_scalar_prefetch=1,
            grid=(1,),
            in_specs=[pl.BlockSpec(memory_space=pl.ANY)] * SIDE,
            out_specs=pl.BlockSpec(memory_space=pl.ANY),
            scratch_shapes=[pltpu.SemaphoreType.DMA((MAX_STRETCHES,))],
        ),
        out_shape=shape,
        compiler_params=pltpu.CompilerParams(vmem_limit_bytes=1024 * 1024),
        cost_estimate=pl.CostEstimate(flops=0, bytes_accessed=2 << 20, transcendentals=0),
        name="pick_home" if home else "pick_visible",
    )(info, *pieces)


def attend_kernel(heads, groups, info, q_hbm, *refs):
    pieces = refs[:SIDE]
    other_hbm, w_hbm = refs[SIDE : SIDE + 2]
    outs = refs[SIDE + 2 : SIDE + 2 + HALVES * groups]
    kv, w, q2, top, acc, att, ready, own_sem, other_sem, q_sem, w_sem, out_sem = refs[SIDE + 2 + HALVES * groups :]
    count = q_hbm.shape[0]
    stretch = kv.shape[1]
    half = stretch // 2
    table = Table(info)
    me = table.me
    slot = table.slot_of(me)
    prompt = slot // MAX_STRETCHES
    mine = lax.rem(slot, MAX_STRETCHES)
    length = table.length(prompt)
    live = mine * stretch < length
    scale = HEAD_DIM ** (-0.5) * LOG2_E
    own_rows = pl.ds(pl.multiple_of(lax.rem(me, 2) * half, half), half)
    other_rows = pl.ds(pl.multiple_of((1 - lax.rem(me, 2)) * half, half), half)
    columns = pl.ds(0, 2 * HEAD_DIM)
    sense = 1 - 2 * (me & 1)
    rows = count // groups
    part_columns = outs[0].shape[1]

    def out_copy(half_index, n):
        target = (table.group + sense * walk(groups)[n]) & (groups - 1)
        source = ready.at[
            pl.ds(pl.multiple_of(target * rows, rows), rows), pl.ds(half_index * part_columns, part_columns)
        ]
        at = half_index * groups + n
        return pltpu.make_async_copy(source, outs[at], out_sem.at[at])

    @pl.when(jnp.logical_not(live))
    def _():
        ready[...] = jnp.zeros_like(ready)
        for half_index in range(HALVES):
            for n in range(groups):
                out_copy(half_index, n).start()

    @pl.when(live)
    def _():
        def q_copy(h):
            return pltpu.make_async_copy(
                q_hbm.at[:, pl.ds(h * HEAD_DIM, HEAD_DIM)], q2.at[pl.ds(h * count, count), :], q_sem.at[h]
            )

        def other_copy(i):
            return pltpu.make_async_copy(other_hbm.at[i], kv.at[i, other_rows, columns], other_sem.at[i])

        def arrive(i):
            pltpu.make_async_copy(pieces[0].at[0], kv.at[i, own_rows, columns], own_sem.at[i]).wait()
            other_copy(i).wait()

        @pl.loop(0, mine + 1)
        def _(i):
            piece, at = held_at(me, table.owner(prompt * MAX_STRETCHES + i))
            start_half(pieces, piece, at, kv.at[i, own_rows, columns], own_sem.at[i])
            other_copy(i).start()

        for h in range(heads):
            q_copy(h).start()
        w_copy = pltpu.make_async_copy(w_hbm, w, w_sem)
        w_copy.start()
        for i in range(MAX_STRETCHES):
            kv[i, :, 2 * HEAD_DIM :] = jnp.ones((stretch, HEAD_DIM), jnp.bfloat16)
        top[...] = jnp.full_like(top, LOW)
        acc[...] = jnp.zeros_like(acc)
        for h in range(heads):
            q_copy(h).wait()
        tile = min(256, count)

        def block(i, diagonal):
            for t in range(heads * count // tile):
                part = slice(t * tile, (t + 1) * tile)
                first = t * tile % count
                seen = first + tile if diagonal else stretch
                scores = lax.dot_general(
                    q2[part, :],
                    kv[i, :seen, :HEAD_DIM],
                    (((1,), (1,)), ((), ())),
                    preferred_element_type=jnp.float32,
                )
                if diagonal:
                    at = lax.broadcasted_iota(jnp.int32, (tile, seen), 0) + first
                    scores = jnp.where(lax.broadcasted_iota(jnp.int32, (tile, seen), 1) <= at, scores, LOW)
                old = top[part, :]
                new = jnp.maximum(old, jnp.max(scores, axis=-1, keepdims=True) * scale)
                weights = jnp.exp2(scores * scale - jnp.concatenate([new] * (seen // HEAD_DIM), axis=1))
                shrink = jnp.exp2(old - new)
                acc[part, :] = acc[part, :] * jnp.concatenate([shrink, shrink], axis=1) + jnp.dot(
                    weights.astype(jnp.bfloat16), kv[i, :seen, HEAD_DIM:], preferred_element_type=jnp.float32
                )
                top[part, :] = new

        @pl.loop(0, mine)
        def _(i):
            arrive(i)
            block(i, False)

        arrive(mine)
        block(mine, True)

        at = mine * stretch + lax.broadcasted_iota(jnp.int32, (count, HEAD_DIM), 0)
        keep = (at < length).astype(jnp.float32)
        for h in range(heads):
            part = slice(h * count, (h + 1) * count)
            att[:, h * HEAD_DIM : (h + 1) * HEAD_DIM] = (
                acc[part, :HEAD_DIM] / acc[part, HEAD_DIM:] * keep
            ).astype(jnp.bfloat16)
        w_copy.wait()
        width = 512
        for half_index in range(HALVES):
            for n in range(part_columns // width):
                columns_at = slice(half_index * part_columns + n * width, half_index * part_columns + (n + 1) * width)
                ready[:, columns_at] = jnp.dot(
                    att[...], w[:, columns_at], preferred_element_type=jnp.float32
                ).astype(jnp.bfloat16)
            for n in range(groups):
                out_copy(half_index, n).start()

    for half_index in range(HALVES):
        for n in range(groups):
            out_copy(half_index, n).wait()


def attend(info, queries, pieces, other, w_out, groups):
    count, columns = queries.shape
    _, half, width = other.shape
    heads = columns // HEAD_DIM
    features = w_out.shape[1]
    return pl.pallas_call(
        functools.partial(attend_kernel, heads, groups),
        grid_spec=pltpu.PrefetchScalarGridSpec(
            num_scalar_prefetch=1,
            grid=(1,),
            in_specs=[pl.BlockSpec(memory_space=pltpu.HBM)]
            + [pl.BlockSpec(memory_space=pl.ANY)] * (SIDE + 1)
            + [pl.BlockSpec(memory_space=pltpu.HBM)],
            out_specs=[pl.BlockSpec(memory_space=pl.ANY)] * (HALVES * groups),
            scratch_shapes=[
                pltpu.VMEM((MAX_STRETCHES, 2 * half, width + HEAD_DIM), jnp.bfloat16),
                pltpu.VMEM(w_out.shape, jnp.bfloat16),
                pltpu.VMEM((heads * count, HEAD_DIM), jnp.bfloat16),
                pltpu.VMEM((heads * count, HEAD_DIM), jnp.float32),
                pltpu.VMEM((heads * count, 2 * HEAD_DIM), jnp.float32),
                pltpu.VMEM((count, columns), jnp.bfloat16),
                pltpu.VMEM((count, features), jnp.bfloat16),
                pltpu.SemaphoreType.DMA((MAX_STRETCHES,)),
                pltpu.SemaphoreType.DMA((MAX_STRETCHES,)),
                pltpu.SemaphoreType.DMA((heads,)),
                pltpu.SemaphoreType.DMA,
                pltpu.SemaphoreType.DMA((HALVES * groups,)),
            ],
        ),
        out_shape=[jax.ShapeDtypeStruct((count // groups, features // HALVES), jnp.bfloat16)] * (HALVES * groups),
        compiler_params=pltpu.CompilerParams(vmem_limit_bytes=38 * 1024 * 1024),
        cost_estimate=pl.CostEstimate(
            flops=2 * count * columns * (features + 4 * MAX_STRETCHES * half), bytes_accessed=16 << 20, transcendentals=0
        ),
        name="attend_rows",
    )(info, queries, *pieces, other, w_out)


def place_kernel(info, *refs):
    pieces = refs[:SIDE]
    other_hbm, keys_ref, values_ref, kv, own_sem, other_sem = refs[SIDE:]
    stretch = kv.shape[1]
    half = stretch // 2
    table = Table(info)
    me = table.me
    prompt = table.homed_at(me, -1)
    homed = prompt >= 0

    @pl.when(jnp.logical_not(homed))
    def _():
        keys_ref[...] = jnp.zeros_like(keys_ref)
        values_ref[...] = jnp.zeros_like(values_ref)

    @pl.when(homed)
    def _():
        own_rows = pl.ds(pl.multiple_of(lax.rem(me, 2) * half, half), half)
        other_rows = pl.ds(pl.multiple_of((1 - lax.rem(me, 2)) * half, half), half)
        length = table.length(prompt)
        for i in range(MAX_STRETCHES):
            piece, slot = held_at(me, table.owner(prompt * MAX_STRETCHES + i))
            start_half(pieces, piece, slot, kv.at[i, own_rows], own_sem.at[i])
            pltpu.make_async_copy(other_hbm.at[i], kv.at[i, other_rows], other_sem.at[i]).start()
        for i in range(MAX_STRETCHES):
            pltpu.make_async_copy(pieces[0].at[0], kv.at[i, own_rows], own_sem.at[i]).wait()
            pltpu.make_async_copy(other_hbm.at[i], kv.at[i, other_rows], other_sem.at[i]).wait()
            live = i * stretch + lax.broadcasted_iota(jnp.int32, (stretch, HEAD_DIM), 0) < length
            rows = slice(i * stretch, (i + 1) * stretch)
            keys_ref[rows, :] = jnp.where(live, kv[i, :, :HEAD_DIM], 0)
            values_ref[rows, :] = jnp.where(live, kv[i, :, HEAD_DIM:], 0)


def place(info, pieces, other):
    _, half, width = other.shape
    rows = MAX_STRETCHES * 2 * half
    cache = jax.ShapeDtypeStruct((rows, HEAD_DIM), jnp.bfloat16)
    return pl.pallas_call(
        place_kernel,
        grid_spec=pltpu.PrefetchScalarGridSpec(
            num_scalar_prefetch=1,
            grid=(1,),
            in_specs=[pl.BlockSpec(memory_space=pl.ANY)] * (SIDE + 1),
            out_specs=[pl.BlockSpec((rows, HEAD_DIM), lambda i, *_: (0, 0))] * 2,
            scratch_shapes=[
                pltpu.VMEM((MAX_STRETCHES, 2 * half, width), jnp.bfloat16),
                pltpu.SemaphoreType.DMA((MAX_STRETCHES,)),
                pltpu.SemaphoreType.DMA((MAX_STRETCHES,)),
            ],
        ),
        out_shape=[cache, cache],
        compiler_params=pltpu.CompilerParams(vmem_limit_bytes=8 * 1024 * 1024),
        cost_estimate=pl.CostEstimate(flops=0, bytes_accessed=4 << 20, transcendentals=0),
        name="place_cache",
    )(info, *pieces, other)


def route(first, step):
    pairs = []
    for x in range(SIDE):
        for y in range(SIDE):
            for core in range(2):
                along_x = (core == 0) == first
                sx, sy = ((x + step) % SIDE, y) if along_x else (x, (y + step) % SIDE)
                pairs.append(((sx * SIDE + sy) * 2 + core, (x * SIDE + y) * 2 + core))
    return pairs


def swap_cores(array):
    return lax.ppermute(array, "sp", [(r, r + 1 - 2 * (r % 2)) for r in range(2 * SIDE * SIDE)])


def gather_halves(keys, values):
    core = lax.axis_index("sp") % 2
    half = keys.shape[0] // 2

    def part(n):
        return jnp.concatenate([lax.dynamic_slice_in_dim(a, n * half, half, 0) for a in (keys, values)], axis=1)

    got = swap_cores(part(1 - core))
    chip = jnp.stack([part(core), got])
    line = jnp.concatenate([chip] + [lax.ppermute(chip, "sp", route(True, step)) for step in range(1, SIDE)], axis=0)
    return [line] + [lax.ppermute(line, "sp", route(False, step)) for step in range(1, SIDE)]


def sum_route(sense, replicas, groups):
    pairs = []
    for r in range(replicas):
        step = sense if r % 2 == 0 else -sense
        pairs += [(r * groups + z, r * groups + (z + step) % groups) for z in range(groups)]
    return pairs


def walk(groups):
    hops = groups // 2
    return list(range(hops, 0, -1)) + list(range(1 - hops, 0)) + [0]


def sum_scattered(blocks, done):
    replicas, groups = lax.axis_size("sp"), lax.axis_size("tp")
    routes = [sum_route(s, replicas, groups) for s in (1, -1)]
    hops = groups // 2

    def hop(walked, block, route):
        if walked is not None:
            block = (block.astype(jnp.float32) + walked.astype(jnp.float32)).astype(jnp.bfloat16)
        return lax.ppermute(block, ("sp", "tp"), route)

    long = short = None
    for k in range(hops):
        long = hop(long, blocks[k], routes[0])
        if k < hops - 1:
            short = hop(short, blocks[hops + k], routes[1])
            if k < hops - 2:
                long, short = lax.optimization_barrier((long, short))
            else:
                long, short, done = lax.optimization_barrier((long, short, done))
    mine = blocks[groups - 1].astype(jnp.float32)
    return (mine + long.astype(jnp.float32) + short.astype(jnp.float32)).astype(jnp.bfloat16), done


def shards(queries, keys, values, w_out, lengths, stretch_owner, home_replica):
    me = lax.axis_index("sp").astype(jnp.int32).reshape(1)
    group = lax.axis_index("tp").astype(jnp.int32).reshape(1)
    groups = lax.axis_size("tp")
    info = jnp.concatenate([me, group, lengths, home_replica, stretch_owner])
    pieces = gather_halves(keys, values)
    visible_other = swap_cores(pick(False, info, pieces))
    blocks = attend(info, queries, pieces, visible_other, w_out, groups)
    later, blocks = lax.optimization_barrier((info, blocks))
    home_other = swap_cores(pick(True, later, pieces))
    caches = place(info, pieces, home_other)
    sums = []
    for h in range(HALVES):
        total, caches = sum_scattered(blocks[h * groups : (h + 1) * groups], caches)
        sums.append(total)
    mixed = jnp.concatenate(sums, axis=1)
    cache_keys, cache_values = caches
    return mixed, cache_keys, cache_values


def solution(mesh):
    placed = (P("sp", "tp"), P("sp", "tp"), P("sp", "tp"), P("tp", None), P(), P(), P())
    return jax.shard_map(
        shards,
        mesh=mesh,
        in_specs=placed,
        out_specs=(P(("sp", "tp"), None), P("sp", "tp"), P("sp", "tp")),
        check_vma=False,
    )
```

```python
import functools

import jax
import jax.numpy as jnp
from jax import lax
from jax.experimental import pallas as pl
from jax.experimental.pallas import tpu as pltpu
from jax.sharding import PartitionSpec as P

HEAD_DIM = 128
MAX_STRETCHES = 8
SIDE = 4
LOG2_E = 1.4426950408889634
LOW = -1e30
HALVES = 2


class Table:
    def __init__(self, ref):
        prompts = (ref.shape[0] - 2) // (MAX_STRETCHES + 2)
        self.me = ref[0]
        self.group = ref[1]
        self.length = lambda p: ref[2 + p]
        self.home = lambda p: ref[2 + prompts + p]
        self.owner = lambda j: ref[2 + 2 * prompts + j]
        self.prompts = prompts

    def slot_of(self, replica):
        return self.find(self.owner, self.prompts * MAX_STRETCHES, replica, 0)

    def homed_at(self, replica, missing):
        return self.find(self.home, self.prompts, replica, missing)

    def find(self, entry, count, wanted, missing):
        return lax.fori_loop(
            0, count, lambda j, found: jnp.where(entry(j) == wanted, j, found), jnp.int32(missing)
        )


def held_at(me, owner):
    bits = SIDE.bit_length() - 1
    dx = ((owner >> (bits + 1)) - (me >> (bits + 1))) & (SIDE - 1)
    dy = ((owner >> 1) - (me >> 1)) & (SIDE - 1)
    other = (owner ^ me) & 1
    first = (me & 1) == 0
    return jnp.where(first, dy, dx), jnp.where(first, dx, dy) * 2 + other


def start_half(pieces, piece, slot, target, sem):
    for p, ref in enumerate(pieces):

        @pl.when(piece == p)
        def _():
            pltpu.make_async_copy(ref.at[slot], target, sem).start()


def pick_kernel(home, info, *refs):
    pieces, out, sem = refs[:SIDE], refs[SIDE], refs[SIDE + 1]
    table = Table(info)
    me = table.me
    other = me ^ 1
    if home:
        prompt = table.homed_at(other, 0)
        count = jnp.int32(MAX_STRETCHES)
    else:
        slot = table.slot_of(other)
        prompt = slot >> (MAX_STRETCHES.bit_length() - 1)
        count = (slot & (MAX_STRETCHES - 1)) + 1

    @pl.loop(0, count)
    def _(i):
        piece, slot = held_at(me, table.owner(prompt * MAX_STRETCHES + i))
        start_half(pieces, piece, slot, out.at[i], sem.at[i])

    @pl.loop(0, count)
    def _(i):
        pltpu.make_async_copy(pieces[0].at[0], out.at[i], sem.at[i]).wait()


def pick(home, info, pieces):
    shape = jax.ShapeDtypeStruct((MAX_STRETCHES,) + pieces[0].shape[1:], jnp.bfloat16)
    return pl.pallas_call(
        functools.partial(pick_kernel, home),
        grid_spec=pltpu.PrefetchScalarGridSpec(
            num_scalar_prefetch=1,
            grid=(1,),
            in_specs=[pl.BlockSpec(memory_space=pl.ANY)] * SIDE,
            out_specs=pl.BlockSpec(memory_space=pl.ANY),
            scratch_shapes=[pltpu.SemaphoreType.DMA((MAX_STRETCHES,))],
        ),
        out_shape=shape,
        compiler_params=pltpu.CompilerParams(vmem_limit_bytes=1024 * 1024),
        cost_estimate=pl.CostEstimate(flops=0, bytes_accessed=2 << 20, transcendentals=0),
        name="pick_home" if home else "pick_visible",
    )(info, *pieces)


def attend_kernel(heads, groups, info, q_hbm, *refs):
    pieces = refs[:SIDE]
    other_hbm, w_hbm = refs[SIDE : SIDE + 2]
    outs = refs[SIDE + 2 : SIDE + 2 + HALVES * groups]
    kv, w, q2, top, acc, att, ready, own_sem, other_sem, q_sem, w_sem, out_sem = refs[SIDE + 2 + HALVES * groups :]
    count = q_hbm.shape[0]
    stretch = kv.shape[1]
    half = stretch // 2
    table = Table(info)
    me = table.me
    slot = table.slot_of(me)
    prompt = slot // MAX_STRETCHES
    mine = lax.rem(slot, MAX_STRETCHES)
    length = table.length(prompt)
    live = mine * stretch < length
    scale = HEAD_DIM ** (-0.5) * LOG2_E
    own_rows = pl.ds(pl.multiple_of(lax.rem(me, 2) * half, half), half)
    other_rows = pl.ds(pl.multiple_of((1 - lax.rem(me, 2)) * half, half), half)
    columns = pl.ds(0, 2 * HEAD_DIM)
    sense = 1 - 2 * (me & 1)
    rows = count // groups
    part_columns = outs[0].shape[1]

    def out_copy(half_index, n):
        target = (table.group + sense * walk(groups)[n]) & (groups - 1)
        source = ready.at[
            pl.ds(pl.multiple_of(target * rows, rows), rows), pl.ds(half_index * part_columns, part_columns)
        ]
        at = half_index * groups + n
        return pltpu.make_async_copy(source, outs[at], out_sem.at[at])

    @pl.when(jnp.logical_not(live))
    def _():
        ready[...] = jnp.zeros_like(ready)
        for half_index in range(HALVES):
            for n in range(groups):
                out_copy(half_index, n).start()

    @pl.when(live)
    def _():
        def q_copy(h):
            return pltpu.make_async_copy(
                q_hbm.at[:, pl.ds(h * HEAD_DIM, HEAD_DIM)], q2.at[pl.ds(h * count, count), :], q_sem.at[h]
            )

        def other_copy(i):
            return pltpu.make_async_copy(other_hbm.at[i], kv.at[i, other_rows, columns], other_sem.at[i])

        def arrive(i):
            pltpu.make_async_copy(pieces[0].at[0], kv.at[i, own_rows, columns], own_sem.at[i]).wait()
            other_copy(i).wait()

        @pl.loop(0, mine + 1)
        def _(i):
            piece, at = held_at(me, table.owner(prompt * MAX_STRETCHES + i))
            start_half(pieces, piece, at, kv.at[i, own_rows, columns], own_sem.at[i])
            other_copy(i).start()

        for h in range(heads):
            q_copy(h).start()
        w_copy = pltpu.make_async_copy(w_hbm, w, w_sem)
        w_copy.start()
        for i in range(MAX_STRETCHES):
            kv[i, :, 2 * HEAD_DIM :] = jnp.ones((stretch, HEAD_DIM), jnp.bfloat16)
        top[...] = jnp.full_like(top, LOW)
        acc[...] = jnp.zeros_like(acc)
        for h in range(heads):
            q_copy(h).wait()
        tile = min(256, count)

        def block(i, diagonal):
            for t in range(heads * count // tile):
                part = slice(t * tile, (t + 1) * tile)
                first = t * tile % count
                seen = first + tile if diagonal else stretch
                scores = lax.dot_general(
                    q2[part, :],
                    kv[i, :seen, :HEAD_DIM],
                    (((1,), (1,)), ((), ())),
                    preferred_element_type=jnp.float32,
                )
                if diagonal:
                    at = lax.broadcasted_iota(jnp.int32, (tile, seen), 0) + first
                    scores = jnp.where(lax.broadcasted_iota(jnp.int32, (tile, seen), 1) <= at, scores, LOW)
                old = top[part, :]
                new = jnp.maximum(old, jnp.max(scores, axis=-1, keepdims=True) * scale)
                weights = jnp.exp2(scores * scale - jnp.concatenate([new] * (seen // HEAD_DIM), axis=1))
                shrink = jnp.exp2(old - new)
                acc[part, :] = acc[part, :] * jnp.concatenate([shrink, shrink], axis=1) + jnp.dot(
                    weights.astype(jnp.bfloat16), kv[i, :seen, HEAD_DIM:], preferred_element_type=jnp.float32
                )
                top[part, :] = new

        @pl.loop(0, mine >> 1)
        def _(j):
            arrive(2 * j)
            arrive(2 * j + 1)
            block(2 * j, False)
            block(2 * j + 1, False)

        @pl.when((mine & 1) == 1)
        def _():
            arrive(mine - 1)
            block(mine - 1, False)

        arrive(mine)
        block(mine, True)

        at = mine * stretch + lax.broadcasted_iota(jnp.int32, (count, HEAD_DIM), 0)
        keep = (at < length).astype(jnp.float32)
        for h in range(heads):
            part = slice(h * count, (h + 1) * count)
            att[:, h * HEAD_DIM : (h + 1) * HEAD_DIM] = (
                acc[part, :HEAD_DIM] / acc[part, HEAD_DIM:] * keep
            ).astype(jnp.bfloat16)
        w_copy.wait()
        width = 512
        for half_index in range(HALVES):
            for n in range(part_columns // width):
                columns_at = slice(half_index * part_columns + n * width, half_index * part_columns + (n + 1) * width)
                ready[:, columns_at] = jnp.dot(
                    att[...], w[:, columns_at], preferred_element_type=jnp.float32
                ).astype(jnp.bfloat16)
            for n in range(groups):
                out_copy(half_index, n).start()

    for half_index in range(HALVES):
        for n in range(groups):
            out_copy(half_index, n).wait()


def attend(info, queries, pieces, other, w_out, groups):
    count, columns = queries.shape
    _, half, width = other.shape
    heads = columns // HEAD_DIM
    features = w_out.shape[1]
    return pl.pallas_call(
        functools.partial(attend_kernel, heads, groups),
        grid_spec=pltpu.PrefetchScalarGridSpec(
            num_scalar_prefetch=1,
            grid=(1,),
            in_specs=[pl.BlockSpec(memory_space=pltpu.HBM)]
            + [pl.BlockSpec(memory_space=pl.ANY)] * (SIDE + 1)
            + [pl.BlockSpec(memory_space=pltpu.HBM)],
            out_specs=[pl.BlockSpec(memory_space=pl.ANY)] * (HALVES * groups),
            scratch_shapes=[
                pltpu.VMEM((MAX_STRETCHES, 2 * half, width + HEAD_DIM), jnp.bfloat16),
                pltpu.VMEM(w_out.shape, jnp.bfloat16),
                pltpu.VMEM((heads * count, HEAD_DIM), jnp.bfloat16),
                pltpu.VMEM((heads * count, HEAD_DIM), jnp.float32),
                pltpu.VMEM((heads * count, 2 * HEAD_DIM), jnp.float32),
                pltpu.VMEM((count, columns), jnp.bfloat16),
                pltpu.VMEM((count, features), jnp.bfloat16),
                pltpu.SemaphoreType.DMA((MAX_STRETCHES,)),
                pltpu.SemaphoreType.DMA((MAX_STRETCHES,)),
                pltpu.SemaphoreType.DMA((heads,)),
                pltpu.SemaphoreType.DMA,
                pltpu.SemaphoreType.DMA((HALVES * groups,)),
            ],
        ),
        out_shape=[jax.ShapeDtypeStruct((count // groups, features // HALVES), jnp.bfloat16)] * (HALVES * groups),
        compiler_params=pltpu.CompilerParams(vmem_limit_bytes=38 * 1024 * 1024),
        cost_estimate=pl.CostEstimate(
            flops=2 * count * columns * (features + 4 * MAX_STRETCHES * half), bytes_accessed=16 << 20, transcendentals=0
        ),
        name="attend_rows",
    )(info, queries, *pieces, other, w_out)


def place_kernel(info, *refs):
    pieces = refs[:SIDE]
    other_hbm, keys_ref, values_ref, kv, own_sem, other_sem = refs[SIDE:]
    stretch = kv.shape[1]
    half = stretch // 2
    table = Table(info)
    me = table.me
    prompt = table.homed_at(me, -1)
    homed = prompt >= 0

    @pl.when(jnp.logical_not(homed))
    def _():
        keys_ref[...] = jnp.zeros_like(keys_ref)
        values_ref[...] = jnp.zeros_like(values_ref)

    @pl.when(homed)
    def _():
        own_rows = pl.ds(pl.multiple_of(lax.rem(me, 2) * half, half), half)
        other_rows = pl.ds(pl.multiple_of((1 - lax.rem(me, 2)) * half, half), half)
        length = table.length(prompt)
        for i in range(MAX_STRETCHES):
            piece, slot = held_at(me, table.owner(prompt * MAX_STRETCHES + i))
            start_half(pieces, piece, slot, kv.at[i, own_rows], own_sem.at[i])
            pltpu.make_async_copy(other_hbm.at[i], kv.at[i, other_rows], other_sem.at[i]).start()
        for i in range(MAX_STRETCHES):
            pltpu.make_async_copy(pieces[0].at[0], kv.at[i, own_rows], own_sem.at[i]).wait()
            pltpu.make_async_copy(other_hbm.at[i], kv.at[i, other_rows], other_sem.at[i]).wait()
            live = i * stretch + lax.broadcasted_iota(jnp.int32, (stretch, HEAD_DIM), 0) < length
            rows = slice(i * stretch, (i + 1) * stretch)
            keys_ref[rows, :] = jnp.where(live, kv[i, :, :HEAD_DIM], 0)
            values_ref[rows, :] = jnp.where(live, kv[i, :, HEAD_DIM:], 0)


def place(info, pieces, other):
    _, half, width = other.shape
    rows = MAX_STRETCHES * 2 * half
    cache = jax.ShapeDtypeStruct((rows, HEAD_DIM), jnp.bfloat16)
    return pl.pallas_call(
        place_kernel,
        grid_spec=pltpu.PrefetchScalarGridSpec(
            num_scalar_prefetch=1,
            grid=(1,),
            in_specs=[pl.BlockSpec(memory_space=pl.ANY)] * (SIDE + 1),
            out_specs=[pl.BlockSpec((rows, HEAD_DIM), lambda i, *_: (0, 0))] * 2,
            scratch_shapes=[
                pltpu.VMEM((MAX_STRETCHES, 2 * half, width), jnp.bfloat16),
                pltpu.SemaphoreType.DMA((MAX_STRETCHES,)),
                pltpu.SemaphoreType.DMA((MAX_STRETCHES,)),
            ],
        ),
        out_shape=[cache, cache],
        compiler_params=pltpu.CompilerParams(vmem_limit_bytes=8 * 1024 * 1024),
        cost_estimate=pl.CostEstimate(flops=0, bytes_accessed=4 << 20, transcendentals=0),
        name="place_cache",
    )(info, *pieces, other)


def route(first, step):
    pairs = []
    for x in range(SIDE):
        for y in range(SIDE):
            for core in range(2):
                along_x = (core == 0) == first
                sx, sy = ((x + step) % SIDE, y) if along_x else (x, (y + step) % SIDE)
                pairs.append(((sx * SIDE + sy) * 2 + core, (x * SIDE + y) * 2 + core))
    return pairs


def swap_cores(array):
    return lax.ppermute(array, "sp", [(r, r + 1 - 2 * (r % 2)) for r in range(2 * SIDE * SIDE)])


def gather_halves(keys, values):
    core = lax.axis_index("sp") % 2
    half = keys.shape[0] // 2

    def part(n):
        return jnp.concatenate([lax.dynamic_slice_in_dim(a, n * half, half, 0) for a in (keys, values)], axis=1)

    got = swap_cores(part(1 - core))
    chip = jnp.stack([part(core), got])
    line = jnp.concatenate([chip] + [lax.ppermute(chip, "sp", route(True, step)) for step in range(1, SIDE)], axis=0)
    return [line] + [lax.ppermute(line, "sp", route(False, step)) for step in range(1, SIDE)]


def sum_route(sense, replicas, groups):
    pairs = []
    for r in range(replicas):
        step = sense if r % 2 == 0 else -sense
        pairs += [(r * groups + z, r * groups + (z + step) % groups) for z in range(groups)]
    return pairs


def walk(groups):
    hops = groups // 2
    return list(range(hops, 0, -1)) + list(range(1 - hops, 0)) + [0]


def sum_scattered(blocks, done):
    replicas, groups = lax.axis_size("sp"), lax.axis_size("tp")
    routes = [sum_route(s, replicas, groups) for s in (1, -1)]
    hops = groups // 2

    def hop(walked, block, route):
        if walked is not None:
            block = (block.astype(jnp.float32) + walked.astype(jnp.float32)).astype(jnp.bfloat16)
        return lax.ppermute(block, ("sp", "tp"), route)

    long = short = None
    for k in range(hops):
        long = hop(long, blocks[k], routes[0])
        if k < hops - 1:
            short = hop(short, blocks[hops + k], routes[1])
            if k < hops - 2:
                long, short = lax.optimization_barrier((long, short))
            else:
                long, short, done = lax.optimization_barrier((long, short, done))
    mine = blocks[groups - 1].astype(jnp.float32)
    return (mine + long.astype(jnp.float32) + short.astype(jnp.float32)).astype(jnp.bfloat16), done


def shards(queries, keys, values, w_out, lengths, stretch_owner, home_replica):
    me = lax.axis_index("sp").astype(jnp.int32).reshape(1)
    group = lax.axis_index("tp").astype(jnp.int32).reshape(1)
    groups = lax.axis_size("tp")
    info = jnp.concatenate([me, group, lengths, home_replica, stretch_owner])
    pieces = gather_halves(keys, values)
    visible_other = swap_cores(pick(False, info, pieces))
    blocks = attend(info, queries, pieces, visible_other, w_out, groups)
    later, blocks = lax.optimization_barrier((info, blocks))
    home_other = swap_cores(pick(True, later, pieces))
    caches = place(info, pieces, home_other)
    sums = []
    for h in range(HALVES):
        total, caches = sum_scattered(blocks[h * groups : (h + 1) * groups], caches)
        sums.append(total)
    mixed = jnp.concatenate(sums, axis=1)
    cache_keys, cache_values = caches
    return mixed, cache_keys, cache_values


def solution(mesh):
    placed = (P("sp", "tp"), P("sp", "tp"), P("sp", "tp"), P("tp", None), P(), P(), P())
    return jax.shard_map(
        shards,
        mesh=mesh,
        in_specs=placed,
        out_specs=(P(("sp", "tp"), None), P("sp", "tp"), P("sp", "tp")),
        check_vma=False,
    )
```
